256 devices in a mesh: blk: 32 (over z_lo, x, core), head: 8 (over z_hi, y).
Axes of the slice: x: 4, y: 4, z: 8 (z_hi: 2, z_lo: 4; z = z_hi * 4 + z_lo), core: 2. Of those that a mesh axis runs over, the one named last changes fastest.
Arguments:
- queries: bfloat16 [4096, 8192], P('blk', 'head'), may hold values from -6 to 6
- key_matrix: bfloat16 [4096, 1024], P(('blk', 'head')), may hold values from -6 to 6
- value_matrix: bfloat16 [4096, 1024], P(('blk', 'head')), may hold values from -6 to 6
- output: bfloat16 [4096, 8192], P('blk', 'head'), may hold values from -6 to 6
- grad_out: bfloat16 [4096, 8192], P('blk', 'head'), may hold values from -6 to 6
- log_norm: bfloat16 [4096, 64], P('blk', 'head'), may hold values from 3 to 6
- doc_ids: int32 [4096], replicated, may hold values from 0 to 5, never falling along the last dimension, each value on 1 to 2048 neighbouring positions
- block_order: int32 [64], replicated, may hold values from 0 to 63, each once
Outputs:
- grad_query: bfloat16 [4096, 8192], P('blk', 'head')
- key_gradient_rows: bfloat16 [4096, 1024], P(('blk', 'head'))
- value_gradient_rows: bfloat16 [4096, 1024], P(('blk', 'head'))
The draws below stay inside these ranges and needn't reach their ends.
Inputs may be any that keep to these rules, and one draw needn't show every extreme that they name: `doc_ids`: never falls along the sequence; each document holds at most 2048 positions, one exactly 2048. `block_order`: each block number once.
All inputs are finite; a program needn't handle non-finite values.
Results may differ from the reference program's by a relative error of at most 0.0058.
Values may be sent and summed in bfloat16 or wider, within the bound.
A program may use at most 64 MiB of HBM per device.

```python
import math
import jax
import jax.numpy as jnp
import numpy as np
from jax import lax

QUERY_HEAD_COUNT = 64
KEY_VALUE_HEADS = 8
HEAD_WIDTH = 128
BLOCK = 64
DOCS = 6
N_BLOCKS = 64
SEQUENCE_TOKENS = 4096
DOC_MAX = 2048


def steps_of(key, dims, shards, least, largest):
    def one(axis_at, blocks):
        draws = jax.random.uniform(jax.random.fold_in(jax.random.fold_in(key, 6), axis_at), (blocks,), jnp.float32, least / len(shards), largest / len(shards))
        return jnp.repeat(jnp.exp(draws), dims[axis_at] // blocks).reshape((-1,) + (1,) * (len(dims) - axis_at - 1))

    loudness = one(*shards[0])
    for cut in shards[1:]:
        loudness = loudness * one(*cut)
    return loudness


def length_profile(number_of, total, bound, skew):
    portions = [(1 << 20) // math.isqrt(grade ** skew) + 1 for grade in range(2, number_of + 1)]
    rest, given = total - bound - (number_of - 1), [1] * (number_of - 1)
    while rest > 0:
        candidates = [i for i in range(number_of - 1) if given[i] < bound]
        mass, remaining = sum([portions[i] for i in candidates]), rest
        for i in candidates:
            extra = min(bound - given[i], max(1, remaining * portions[i] // mass), rest)
            given[i] = given[i] + extra
            rest = rest - extra
    return np.array([bound] + given)


def ragged_sizes(stream_key, count, total, bound, skew):
    if count == 2:
        one = jax.random.randint(stream_key, (), max(1, total - bound), min(bound, total - 1) + 1)
        return jnp.stack([one, total - one])
    tallies = jnp.asarray(length_profile(count, total, bound, skew), jnp.int32)
    couples = (count - 1) // 2
    source_of, taker = tallies[1:1 + 2 * couples:2], tallies[2:2 + 2 * couples:2]
    margin = jnp.minimum(source_of - 1, bound - taker)
    passed = jax.random.randint(jax.random.fold_in(stream_key, 1), (couples,), 0, 1 << 20) % (margin + 1)
    tallies = tallies.at[1:1 + 2 * couples:2].set(source_of - passed).at[2:2 + 2 * couples:2].set(taker + passed)
    return tallies[jax.random.permutation(jax.random.fold_in(stream_key, 2), count)]


def normal_values(key, extent, deviation, reach, split=(), held_as=jnp.bfloat16):
    entries = jax.random.normal(key, extent, jnp.float32) * deviation
    if len(split) > 0:
        entries = steps_of(key, extent, split, -0.22, 0.18) * entries
    return jnp.clip(entries, min=-reach, max=reach).astype(held_as)


def setup_inputs(seed: int = 0) -> dict:
    arg_keys = jax.random.split(jax.random.key(seed), 9)
    return {
        "queries": normal_values(arg_keys[0], (SEQUENCE_TOKENS, QUERY_HEAD_COUNT * HEAD_WIDTH), 1.0, 6.0, ((0, 32), (1, 8))),
        "key_matrix": normal_values(arg_keys[1], (SEQUENCE_TOKENS, KEY_VALUE_HEADS * HEAD_WIDTH), 1.0, 6.0, ((0, 256),)),
        "value_matrix": normal_values(arg_keys[2], (SEQUENCE_TOKENS, KEY_VALUE_HEADS * HEAD_WIDTH), 1.0, 6.0, ((0, 256),)),
        "output": normal_values(arg_keys[3], (SEQUENCE_TOKENS, QUERY_HEAD_COUNT * HEAD_WIDTH), 1.0, 6.0, ((0, 32), (1, 8))),
        "grad_out": normal_values(arg_keys[4], (SEQUENCE_TOKENS, QUERY_HEAD_COUNT * HEAD_WIDTH), 1.0, 6.0, ((0, 32), (1, 8))),
        "log_norm": jnp.clip(3.0 + 3.0 * jax.random.uniform(arg_keys[5], (SEQUENCE_TOKENS, QUERY_HEAD_COUNT), jnp.float32) ** steps_of(arg_keys[5], (SEQUENCE_TOKENS, QUERY_HEAD_COUNT), ((0, 32), (1, 8)), -0.2, 0.2), 3.0, 6.0).astype(jnp.bfloat16),
        "doc_ids": jnp.searchsorted(jnp.cumsum(ragged_sizes(arg_keys[6], DOCS, SEQUENCE_TOKENS, DOC_MAX, 2)), jnp.arange(SEQUENCE_TOKENS), side="right").astype(jnp.int32),
        "block_order": jax.random.permutation(arg_keys[7], N_BLOCKS).astype(jnp.int32),
    }


def stored_layout(doc_ids, block_order):
    row_index = jnp.arange(SEQUENCE_TOKENS, dtype=jnp.int32)
    positions = block_order[row_index // BLOCK] * BLOCK + row_index % BLOCK
    return (positions, doc_ids[positions])

def reference(queries, key_matrix, value_matrix, output, grad_out, log_norm, doc_ids, block_order):
    softmax_scale = 1.0 / math.sqrt(HEAD_WIDTH)
    group_width = QUERY_HEAD_COUNT // KEY_VALUE_HEADS
    positions, documents = stored_layout(doc_ids, block_order)
    allowed = (positions[None, :] <= positions[:, None]) & (documents[None, :] == documents[:, None])
    query_heads = queries.reshape(SEQUENCE_TOKENS, QUERY_HEAD_COUNT, HEAD_WIDTH)
    heads_of_keys = key_matrix.reshape(SEQUENCE_TOKENS, KEY_VALUE_HEADS, HEAD_WIDTH)
    heads_of_values = value_matrix.reshape(SEQUENCE_TOKENS, KEY_VALUE_HEADS, HEAD_WIDTH)
    grad_heads = grad_out.reshape(SEQUENCE_TOKENS, QUERY_HEAD_COUNT, HEAD_WIDTH)
    row_delta = lax.optimization_barrier(jnp.sum(grad_heads.astype(jnp.float32) * output.reshape(SEQUENCE_TOKENS, QUERY_HEAD_COUNT, HEAD_WIDTH).astype(jnp.float32), axis=-1))

    def one_head(head_index):
        kv_index = head_index // group_width
        query_one = lax.dynamic_index_in_dim(query_heads, head_index, 1, keepdims=False)
        grad_one = lax.dynamic_index_in_dim(grad_heads, head_index, 1, keepdims=False)
        key_one = lax.dynamic_index_in_dim(heads_of_keys, kv_index, 1, keepdims=False)
        value_one = lax.dynamic_index_in_dim(heads_of_values, kv_index, 1, keepdims=False)
        norm_one = lax.dynamic_index_in_dim(log_norm, head_index, 1, keepdims=False).astype(jnp.float32)
        delta_one = lax.dynamic_index_in_dim(row_delta, head_index, 1, keepdims=False)
        scores = jnp.dot(query_one, key_one.T, preferred_element_type=jnp.float32) * softmax_scale
        weights = jnp.where(allowed, jnp.exp(scores - norm_one[:, None]), 0.0)
        grad_weights = jnp.dot(grad_one, value_one.T, preferred_element_type=jnp.float32)
        grad_scores = weights * (grad_weights - delta_one[:, None])
        weights_b = weights.astype(jnp.bfloat16)
        scores_b = grad_scores.astype(jnp.bfloat16)
        grad_value_one = jnp.dot(weights_b.T, grad_one, preferred_element_type=jnp.float32)
        grad_key_one = jnp.dot(scores_b.T, query_one, preferred_element_type=jnp.float32) * softmax_scale
        grad_query_one = jnp.dot(scores_b, key_one, preferred_element_type=jnp.float32) * softmax_scale
        return (grad_query_one, grad_key_one, grad_value_one)
    grad_query, key_gradient, value_gradient = lax.map(one_head, jnp.arange(QUERY_HEAD_COUNT, dtype=jnp.int32))
    grad_query = jnp.transpose(grad_query, (1, 0, 2)).reshape(SEQUENCE_TOKENS, QUERY_HEAD_COUNT * HEAD_WIDTH).astype(jnp.bfloat16)
    key_gradient = lax.optimization_barrier(jnp.sum(key_gradient.reshape(KEY_VALUE_HEADS, group_width, SEQUENCE_TOKENS, HEAD_WIDTH), axis=1))
    value_gradient = lax.optimization_barrier(jnp.sum(value_gradient.reshape(KEY_VALUE_HEADS, group_width, SEQUENCE_TOKENS, HEAD_WIDTH), axis=1))
    key_gradient_rows = jnp.transpose(key_gradient, (1, 0, 2)).reshape(SEQUENCE_TOKENS, KEY_VALUE_HEADS * HEAD_WIDTH).astype(jnp.bfloat16)
    value_gradient_rows = jnp.transpose(value_gradient, (1, 0, 2)).reshape(SEQUENCE_TOKENS, KEY_VALUE_HEADS * HEAD_WIDTH).astype(jnp.bfloat16)
    return (grad_query, key_gradient_rows, value_gradient_rows)
```

```python
import functools
import math

import jax
import jax.numpy as jnp
from jax import lax
from jax.experimental import pallas as pl
from jax.experimental.pallas import tpu as pltpu
from jax.sharding import PartitionSpec as P

WIDTH = 128
BLOCK = 64
DOCS = 6
TILE = 256
MASKED = -(2.0**17)
ROOT = math.sqrt(WIDTH)
SCALE = 1.0 / ROOT
EXP2_SCALE = SCALE * math.log2(math.e)
BF16 = jnp.bfloat16
F32 = jnp.float32


def root_parts():
    parts, rest = [], ROOT
    for _ in range(3):
        term = _to_bf16(rest)
        parts.append(term)
        rest -= term
    return parts


def _to_bf16(value):
    mantissa, exponent = math.frexp(value)
    return math.ldexp(round(mantissa * 256), exponent - 8)


ROOT_PARTS = root_parts()


def attend_kernel(
    span_ref, order_ref, docs_ref, q_ref, o_ref, g_ref, norm_ref, kv_ref,
    dq_ref, dkv_ref,
    k_pos, v_pos, dk_acc, dv_acc, q_all, g_all, q_turn, g_turn, dq_turn,
):
    rows = 8 * BLOCK
    blocks = k_pos.shape[0] // BLOCK

    def sort_block(i, carry):
        at = pl.multiple_of(order_ref[i] * BLOCK, BLOCK)
        half = pl.multiple_of((i % 2) * BLOCK, BLOCK)
        k_pos[pl.ds(at, BLOCK), :] = kv_ref[i // 2, 0, pl.ds(half, BLOCK), :]
        v_pos[pl.ds(at, BLOCK), :] = kv_ref[i // 2, 1, pl.ds(half, BLOCK), :]
        return carry

    lax.fori_loop(0, blocks, sort_block, 0, unroll=4)
    dk_acc[...] = jnp.zeros_like(dk_acc)
    dv_acc[...] = jnp.zeros_like(dv_acc)

    docs = docs_ref[...]
    starts = [jnp.sum((docs < d).astype(jnp.int32)) for d in range(1, DOCS)]

    lane = lax.broadcasted_iota(jnp.int32, (BLOCK, WIDTH), 1)
    row = lax.broadcasted_iota(jnp.int32, (BLOCK, WIDTH), 0)
    one_hot = (lane == row).astype(F32)
    norm_lane = (lane >= BLOCK) & (lane < BLOCK + 3)

    tile_lane = lax.broadcasted_iota(jnp.int32, (TILE, WIDTH), 1)
    tile_row = lax.broadcasted_iota(jnp.int32, (TILE, WIDTH), 0)
    value_extra = jnp.where(tile_lane < 3, -1.0, 0.0).astype(BF16)
    norm_extra = jnp.zeros((TILE, WIDTH), F32)
    for i, part in enumerate(ROOT_PARTS):
        norm_extra = jnp.where(tile_lane == BLOCK + i, -part, norm_extra)

    for half in range(2):
        here = slice(half * BLOCK, (half + 1) * BLOCK)
        for h in range(8):
            cols = slice(h * WIDTH, (h + 1) * WIDTH)
            there = slice(h * BLOCK, (h + 1) * BLOCK)
            g = g_ref[here, cols]
            q_all[half, there, :WIDTH] = q_ref[here, cols]
            g_all[half, there, :WIDTH] = g
            norm = norm_ref[here, h : h + 1].astype(F32)
            q_all[half, there, WIDTH:] = jnp.where(norm_lane, norm, one_hot).astype(BF16)
            delta = jnp.sum(g.astype(F32) * o_ref[here, cols].astype(F32), axis=1, keepdims=True)
            high = delta.astype(BF16).astype(F32)
            mid = (delta - high).astype(BF16).astype(F32)
            low = delta - high - mid
            extra = jnp.where(
                lane == 0, high, jnp.where(lane == 1, mid, jnp.where(lane == 2, low, 0.0))
            )
            g_all[half, there, WIDTH:] = extra.astype(BF16)
        q_turn[half] = q_all[half].T
        g_turn[half] = g_all[half].T

        p = order_ref[2 * span_ref[0] + half]
        first = p * BLOCK
        first_doc = jnp.int32(0)
        for s in starts:
            first_doc = jnp.maximum(first_doc, jnp.where(s <= first, s, 0))
        query_pos = tile_lane + first
        query_start = jnp.zeros_like(query_pos)
        for s in starts:
            query_start = jnp.maximum(query_start, jnp.where(s <= query_pos, s, 0))
        dq_turn[...] = jnp.zeros_like(dq_turn)

        def visit(t, carry):
            at = pl.multiple_of(t * TILE, TILE)
            tile = pl.ds(at, TILE)
            keys = k_pos[tile, :]
            key_pos = tile_row + at
            hidden = ((key_pos > query_pos) | (key_pos < query_start)) & (tile_lane < BLOCK)
            extra = jnp.where(hidden, MASKED, norm_extra).astype(BF16)
            scores = jnp.dot(
                jnp.concatenate([keys, extra], axis=1), q_turn[half],
                preferred_element_type=F32,
            )
            weights = jnp.exp2(scores * EXP2_SCALE)
            grad_weights = jnp.dot(
                jnp.concatenate([v_pos[tile, :], value_extra], axis=1), g_turn[half],
                preferred_element_type=F32,
            )
            grad_scores = (weights * grad_weights).astype(BF16)
            dv_acc[tile, :] += jnp.dot(
                weights.astype(BF16), g_all[half, :, :WIDTH], preferred_element_type=F32
            )
            dk_acc[tile, :] += jnp.dot(
                grad_scores, q_all[half, :, :WIDTH], preferred_element_type=F32
            )
            dq_turn[...] += jnp.dot(keys.T, grad_scores, preferred_element_type=F32)
            return carry

        lax.fori_loop(first_doc // TILE, first // TILE + 1, visit, 0)
        dq = (dq_turn[...] * SCALE).T
        for h in range(8):
            dq_ref[here, h * WIDTH : (h + 1) * WIDTH] = dq[h * BLOCK : (h + 1) * BLOCK].astype(BF16)

    def store_block(i, carry):
        at = pl.multiple_of(order_ref[i] * BLOCK, BLOCK)
        half = pl.multiple_of((i % 2) * BLOCK, BLOCK)
        dkv_ref[i // 2, 0, pl.ds(half, BLOCK), :] = (
            dk_acc[pl.ds(at, BLOCK), :] * SCALE
        ).astype(dkv_ref.dtype)
        dkv_ref[i // 2, 1, pl.ds(half, BLOCK), :] = dv_acc[pl.ds(at, BLOCK), :].astype(
            dkv_ref.dtype
        )
        return carry

    lax.fori_loop(0, blocks, store_block, 0, unroll=4)


def attend(span, order, docs, queries, output, grad_out, log_norm, kv, grad_dtype):
    spans, _, span_rows, _ = kv.shape
    length = spans * span_rows
    smem = pl.BlockSpec(memory_space=pltpu.SMEM)
    vmem = pl.BlockSpec(memory_space=pltpu.VMEM)
    return pl.pallas_call(
        attend_kernel,
        out_shape=(
            jax.ShapeDtypeStruct(queries.shape, BF16),
            jax.ShapeDtypeStruct(kv.shape, grad_dtype),
        ),
        in_specs=[smem, smem] + [vmem] * 6,
        out_specs=(vmem, vmem),
        scratch_shapes=[
            pltpu.VMEM((length, WIDTH), BF16),
            pltpu.VMEM((length, WIDTH), BF16),
            pltpu.VMEM((length, WIDTH), F32),
            pltpu.VMEM((length, WIDTH), F32),
            pltpu.VMEM((2, 8 * BLOCK, 2 * WIDTH), BF16),
            pltpu.VMEM((2, 8 * BLOCK, 2 * WIDTH), BF16),
            pltpu.VMEM((2, 2 * WIDTH, 8 * BLOCK), BF16),
            pltpu.VMEM((2, 2 * WIDTH, 8 * BLOCK), BF16),
            pltpu.VMEM((WIDTH, 8 * BLOCK), F32),
        ],
        compiler_params=pltpu.CompilerParams(vmem_limit_bytes=48 * 2**20),
        name="attend",
    )(span, order, docs, queries, output, grad_out, log_norm, kv)


def body(queries, key_matrix, value_matrix, output, grad_out, log_norm, doc_ids, block_order):
    span = lax.axis_index("blk").astype(jnp.int32).reshape(1)
    both = jnp.stack([key_matrix, value_matrix])
    rows_here = lax.all_to_all(both, "head", split_axis=2, concat_axis=1, tiled=True)
    kv = lax.all_gather(rows_here, "blk", axis=0, tiled=False)
    grad_query, grad_kv = attend(
        span, block_order, doc_ids.reshape(-1, WIDTH), queries, output, grad_out, log_norm, kv, F32
    )
    grad_here = lax.psum_scatter(grad_kv, "blk", scatter_dimension=0, tiled=False).astype(BF16)
    back = lax.all_to_all(grad_here, "head", split_axis=1, concat_axis=2, tiled=True)
    return (grad_query, back[0], back[1])


def solution(mesh):
    placed = (
        P("blk", "head"),
        P(("blk", "head"), None),
        P(("blk", "head"), None),
        P("blk", "head"),
        P("blk", "head"),
        P("blk", "head"),
        P(),
        P(),
    )
    return jax.shard_map(
        body,
        mesh=mesh,
        in_specs=placed,
        out_specs=(P("blk", "head"), P(("blk", "head"), None), P(("blk", "head"), None)),
        check_vma=False,
    )
```

```python
import functools
import math

import jax
import jax.numpy as jnp
from jax import lax
from jax.experimental import pallas as pl
from jax.experimental.pallas import tpu as pltpu
from jax.sharding import PartitionSpec as P

WIDTH = 128
BLOCK = 64
DOCS = 6
TILE = 256
MASKED = -(2.0**17)
ROOT = math.sqrt(WIDTH)
SCALE = 1.0 / ROOT
EXP2_SCALE = SCALE * math.log2(math.e)
BF16 = jnp.bfloat16
F32 = jnp.float32


def root_parts():
    parts, rest = [], ROOT
    for _ in range(3):
        term = _to_bf16(rest)
        parts.append(term)
        rest -= term
    return parts


def _to_bf16(value):
    mantissa, exponent = math.frexp(value)
    return math.ldexp(round(mantissa * 256), exponent - 8)


ROOT_PARTS = root_parts()


def attend_kernel(
    span_ref, order_ref, docs_ref, q_ref, o_ref, g_ref, norm_ref, kv_ref,
    dq_ref, dkv_ref,
    k_pos, v_pos, dk_acc, dv_acc, q_all, g_all, q_turn, g_turn, dq_turn,
):
    rows = 8 * BLOCK
    blocks = k_pos.shape[0] // BLOCK

    def sort_block(i, carry):
        at = pl.multiple_of(order_ref[i] * BLOCK, BLOCK)
        half = pl.multiple_of((i % 2) * BLOCK, BLOCK)
        k_pos[pl.ds(at, BLOCK), :] = kv_ref[i // 2, 0, pl.ds(half, BLOCK), :]
        v_pos[pl.ds(at, BLOCK), :] = kv_ref[i // 2, 1, pl.ds(half, BLOCK), :]
        return carry

    lax.fori_loop(0, blocks, sort_block, 0, unroll=4)
    dk_acc[...] = jnp.zeros_like(dk_acc)
    dv_acc[...] = jnp.zeros_like(dv_acc)

    docs = docs_ref[...]
    starts = [jnp.sum((docs < d).astype(jnp.int32)) for d in range(1, DOCS)]

    lane = lax.broadcasted_iota(jnp.int32, (BLOCK, WIDTH), 1)
    row = lax.broadcasted_iota(jnp.int32, (BLOCK, WIDTH), 0)
    one_hot = (lane == row).astype(F32)
    norm_lane = (lane >= BLOCK) & (lane < BLOCK + 3)

    tile_lane = lax.broadcasted_iota(jnp.int32, (TILE, WIDTH), 1)
    tile_row = lax.broadcasted_iota(jnp.int32, (TILE, WIDTH), 0)
    value_extra = jnp.where(tile_lane < 3, -1.0, 0.0).astype(BF16)
    norm_extra = jnp.zeros((TILE, WIDTH), F32)
    for i, part in enumerate(ROOT_PARTS):
        norm_extra = jnp.where(tile_lane == BLOCK + i, -part, norm_extra)

    for half in range(2):
        here = slice(half * BLOCK, (half + 1) * BLOCK)
        for h in range(8):
            cols = slice(h * WIDTH, (h + 1) * WIDTH)
            there = slice(h * BLOCK, (h + 1) * BLOCK)
            g = g_ref[here, cols]
            q_all[half, there, :WIDTH] = q_ref[here, cols]
            g_all[half, there, :WIDTH] = g
            norm = norm_ref[here, h : h + 1].astype(F32)
            q_all[half, there, WIDTH:] = jnp.where(norm_lane, norm, one_hot).astype(BF16)
            delta = jnp.sum(g.astype(F32) * o_ref[here, cols].astype(F32), axis=1, keepdims=True)
            high = delta.astype(BF16).astype(F32)
            mid = (delta - high).astype(BF16).astype(F32)
            low = delta - high - mid
            extra = jnp.where(
                lane == 0, high, jnp.where(lane == 1, mid, jnp.where(lane == 2, low, 0.0))
            )
            g_all[half, there, WIDTH:] = extra.astype(BF16)
        q_turn[half] = q_all[half].T
        g_turn[half] = g_all[half].T

        p = order_ref[2 * span_ref[0] + half]
        first = p * BLOCK
        first_doc = jnp.int32(0)
        for s in starts:
            first_doc = jnp.maximum(first_doc, jnp.where(s <= first, s, 0))
        query_pos = tile_lane + first
        query_start = jnp.zeros_like(query_pos)
        for s in starts:
            query_start = jnp.maximum(query_start, jnp.where(s <= query_pos, s, 0))
        dq_turn[...] = jnp.zeros_like(dq_turn)

        def visit(t, carry):
            at = pl.multiple_of(t * TILE, TILE)
            tile = pl.ds(at, TILE)
            keys = k_pos[tile, :]
            key_pos = tile_row + at
            hidden = ((key_pos > query_pos) | (key_pos < query_start)) & (tile_lane < BLOCK)
            extra = jnp.where(hidden, MASKED, norm_extra).astype(BF16)
            scores = jnp.dot(
                jnp.concatenate([keys, extra], axis=1), q_turn[half],
                preferred_element_type=F32,
            )
            weights = jnp.exp2(scores * EXP2_SCALE)
            grad_weights = jnp.dot(
                jnp.concatenate([v_pos[tile, :], value_extra], axis=1), g_turn[half],
                preferred_element_type=F32,
            )
            grad_scores = (weights * grad_weights).astype(BF16)
            dv_acc[tile, :] += jnp.dot(
                weights.astype(BF16), g_all[half, :, :WIDTH], preferred_element_type=F32
            )
            dk_acc[tile, :] += jnp.dot(
                grad_scores, q_all[half, :, :WIDTH], preferred_element_type=F32
            )
            dq_turn[...] += jnp.dot(keys.T, grad_scores, preferred_element_type=F32)
            return carry

        lax.fori_loop(first_doc // TILE, first // TILE + 1, visit, 0)
        dq = (dq_turn[...] * SCALE).T
        for h in range(8):
            dq_ref[here, h * WIDTH : (h + 1) * WIDTH] = dq[h * BLOCK : (h + 1) * BLOCK].astype(BF16)

    def store_block(i, carry):
        at = pl.multiple_of(order_ref[i] * BLOCK, BLOCK)
        half = pl.multiple_of((i % 2) * BLOCK, BLOCK)
        dkv_ref[i // 2, 0, pl.ds(half, BLOCK), :] = (
            dk_acc[pl.ds(at, BLOCK), :] * SCALE
        ).astype(dkv_ref.dtype)
        dkv_ref[i // 2, 1, pl.ds(half, BLOCK), :] = dv_acc[pl.ds(at, BLOCK), :].astype(
            dkv_ref.dtype
        )
        return carry

    lax.fori_loop(0, blocks, store_block, 0, unroll=4)


def attend(span, order, docs, queries, output, grad_out, log_norm, kv, grad_dtype):
    spans, _, span_rows, _ = kv.shape
    length = spans * span_rows
    smem = pl.BlockSpec(memory_space=pltpu.SMEM)
    vmem = pl.BlockSpec(memory_space=pltpu.VMEM)
    return pl.pallas_call(
        attend_kernel,
        out_shape=(
            jax.ShapeDtypeStruct(queries.shape, BF16),
            jax.ShapeDtypeStruct(kv.shape, grad_dtype),
        ),
        in_specs=[smem, smem] + [vmem] * 6,
        out_specs=(vmem, vmem),
        scratch_shapes=[
            pltpu.VMEM((length, WIDTH), BF16),
            pltpu.VMEM((length, WIDTH), BF16),
            pltpu.VMEM((length, WIDTH), F32),
            pltpu.VMEM((length, WIDTH), F32),
            pltpu.VMEM((2, 8 * BLOCK, 2 * WIDTH), BF16),
            pltpu.VMEM((2, 8 * BLOCK, 2 * WIDTH), BF16),
            pltpu.VMEM((2, 2 * WIDTH, 8 * BLOCK), BF16),
            pltpu.VMEM((2, 2 * WIDTH, 8 * BLOCK), BF16),
            pltpu.VMEM((WIDTH, 8 * BLOCK), F32),
        ],
        compiler_params=pltpu.CompilerParams(vmem_limit_bytes=48 * 2**20),
        name="attend",
    )(span, order, docs, queries, output, grad_out, log_norm, kv)


class Place:
    def __init__(self):
        self.span = lax.axis_index("blk")
        self.head = lax.axis_index("head")
        self.core = self.span % 2
        self.x = (self.span // 2) % 4
        self.z = self.span // 8
        self.near_z = (1 + self.z % 2, (2 + 3 * self.z) % 5, 3 * (1 - self.z // 2))

    def at(self, z, dx=0, other=False):
        core = 1 - self.core if other else self.core
        return (z * 4 + (self.x + dx) % 4) * 2 + core

    @property
    def sibling(self):
        return self.at(self.z, 0, True)


def meet(place):
    barrier = pltpu.get_barrier_semaphore()
    peers = [(place.span, (place.head + d) % 8) for d in range(1, 8)]
    peers += [(place.at(z), place.head) for z in place.near_z]
    peers += [(place.at(place.z, 1), place.head), (place.at(place.z, 3), place.head)]
    peers += [(place.sibling, place.head)]
    for peer in peers:
        pl.semaphore_signal(
            barrier, inc=1, device_id=peer, device_id_type=pl.DeviceIdType.MESH
        )
    pl.semaphore_wait(barrier, len(peers))


def copy_to(src, dst, send, recv, span, head):
    return pltpu.make_async_remote_copy(
        src_ref=src, dst_ref=dst, send_sem=send, recv_sem=recv,
        device_id=(span, head), device_id_type=pl.DeviceIdType.MESH,
    )


def head_rows(head):
    return pl.ds(pl.multiple_of(head * 16, 16), 16)


def head_columns(head):
    return pl.ds(pl.multiple_of(head * WIDTH, WIDTH), WIDTH)


def gather_kernel(
    k_ref, v_ref, kv_ref,
    head_send, head_recv, z_send, z_recv, x_send, x_recv, f_send, f_recv, s_send, s_recv,
):
    me = Place()
    own, head = me.span, me.head
    meet(me)
    sent = []

    def send(*args):
        copy = copy_to(*args)
        copy.start()
        sent.append(copy)

    for d in range(1, 8):
        peer = (head + d) % 8
        for j, ref in enumerate((k_ref, v_ref)):
            send(
                ref.at[:, head_columns(peer)], kv_ref.at[own, j, head_rows(head), :],
                head_send.at[j, d], head_recv.at[j, d], own, peer,
            )
    for j, ref in enumerate((k_ref, v_ref)):
        kv_ref[own, j, head_rows(head), :] = ref[:, head_columns(head)]
    for d in range(1, 8):
        peer = (head + 8 - d) % 8
        for j in range(2):
            here = kv_ref.at[own, j, head_rows(peer), :]
            copy_to(here, here, head_send.at[j, d], head_recv.at[j, d], own, peer).wait_recv()

    order = (me.z,) + me.near_z
    left, right, sibling = me.at(me.z, 3), me.at(me.z, 1), me.sibling

    def arrived(part, recv, span):
        copy_to(part, part, s_send.at[0, 0], recv, span, head).wait_recv()

    def over(part, k, which):
        send(part, part, s_send.at[k, which], s_recv.at[k, which], sibling, head)

    def column(k):
        span = me.at(order[k])
        block = kv_ref.at[span]
        if k > 0:
            arrived(block, z_recv.at[order[k]], span)
        send(block, block, x_send.at[0, k], x_recv.at[0, k], right, head)
        send(block, block, x_send.at[1, k], x_recv.at[1, k], left, head)
        if k == 0:
            for i, z in enumerate(me.near_z):
                send(block, block, z_send.at[i], z_recv.at[me.z], me.at(z), head)
        over(block, k, 0)

    def beside(k):
        block = kv_ref.at[me.at(order[k], 3)]
        arrived(block, x_recv.at[0, k], left)
        send(block.at[0], block.at[0], f_send.at[0, k], f_recv.at[0, k], right, head)
        over(block, k, 1)
        block = kv_ref.at[me.at(order[k], 1)]
        arrived(block, x_recv.at[1, k], right)
        send(block.at[1], block.at[1], f_send.at[1, k], f_recv.at[1, k], left, head)
        over(block, k, 2)

    def across(k):
        block = kv_ref.at[me.at(order[k], 2)]
        arrived(block.at[0], f_recv.at[0, k], left)
        over(block.at[0], k, 3)
        arrived(block.at[1], f_recv.at[1, k], right)
        over(block.at[1], k, 4)

    column(0)
    column(1)
    beside(0)
    column(2)
    beside(1)
    across(0)
    column(3)
    beside(2)
    across(1)
    beside(3)
    across(2)
    across(3)
    for k in range(4):
        for which, dx in enumerate((0, 3, 1)):
            arrived(kv_ref.at[me.at(order[k], dx, True)], s_recv.at[k, which], sibling)
        block = kv_ref.at[me.at(order[k], 2, True)]
        arrived(block.at[0], s_recv.at[k, 3], sibling)
        arrived(block.at[1], s_recv.at[k, 4], sibling)
    for copy in sent:
        copy.wait_send()


def gather(key_matrix, value_matrix):
    vmem = pl.BlockSpec(memory_space=pltpu.VMEM)
    dma = pltpu.SemaphoreType.DMA
    return pl.pallas_call(
        gather_kernel,
        out_shape=jax.ShapeDtypeStruct((32, 2, 2 * BLOCK, WIDTH), BF16),
        in_specs=[vmem, vmem],
        out_specs=vmem,
        scratch_shapes=[
            dma((2, 8)), dma((2, 8)), dma((3,)), dma((4,)), dma((2, 4)), dma((2, 4)),
            dma((2, 4)), dma((2, 4)), dma((4, 5)), dma((4, 5)),
        ],
        compiler_params=pltpu.CompilerParams(
            collective_id=0, has_side_effects=True, vmem_limit_bytes=32 * 2**20
        ),
        name="gather",
    )(key_matrix, value_matrix)


def scatter_kernel(
    part_ref, dk_ref, dv_ref,
    sib, far, near, deep, far_out, near_out, deep_out, total,
    s_send, s_recv, f_send, f_recv, x_send, x_recv, z_send, z_recv, head_send, head_recv,
):
    me = Place()
    own, head = me.span, me.head
    meet(me)
    sent = []

    def send(*args):
        copy = copy_to(*args)
        copy.start()
        sent.append(copy)

    def arrived(part, recv, span):
        copy_to(part, part, s_send.at[0, 0], recv, span, head).wait_recv()

    order = me.near_z[::-1] + (me.z,)
    left, right, sibling = me.at(me.z, 3), me.at(me.z, 1), me.sibling
    for k in range(4):
        for dx in (2, 1, 3, 0):
            send(
                part_ref.at[me.at(order[k], dx, True)], sib.at[k, dx],
                s_send.at[k, dx], s_recv.at[k, dx], sibling, head,
            )

    def pair(k, dx, j):
        return part_ref[me.at(order[k], dx), j].astype(F32) + sib[k, dx, j].astype(F32)

    def across(k):
        arrived(sib.at[k, 2], s_recv.at[k, 2], sibling)
        for j, span in enumerate((right, left)):
            far_out[k, j] = pair(k, 2, j).astype(BF16)
            send(far_out.at[k, j], far.at[j, k], f_send.at[j, k], f_recv.at[j, k], span, head)

    def beside(k):
        for i, (dx, span, source) in enumerate(((1, right, left), (3, left, right))):
            arrived(sib.at[k, dx], s_recv.at[k, dx], sibling)
            arrived(far.at[i, k], f_recv.at[i, k], source)
            near_out[i, k, i] = (pair(k, dx, i) + far[i, k].astype(F32)).astype(BF16)
            near_out[i, k, 1 - i] = pair(k, dx, 1 - i).astype(BF16)
            send(near_out.at[i, k], near.at[i, k], x_send.at[i, k], x_recv.at[i, k], span, head)

    def column(k):
        arrived(sib.at[k, 0], s_recv.at[k, 0], sibling)
        arrived(near.at[0, k], x_recv.at[0, k], left)
        arrived(near.at[1, k], x_recv.at[1, k], right)
        sums = [
            pair(k, 0, j) + near[0, k, j].astype(F32) + near[1, k, j].astype(F32)
            for j in range(2)
        ]
        if k == 3:
            return sums
        for j in range(2):
            deep_out[k, j] = sums[j].astype(BF16)
        send(
            deep_out.at[k], deep.at[me.z], z_send.at[k], z_recv.at[me.z], me.at(order[k]), head
        )

    for k in range(4):
        across(k)
    beside(0)
    beside(1)
    column(0)
    beside(2)
    column(1)
    beside(3)
    column(2)
    sums = column(3)
    for z in me.near_z:
        arrived(deep.at[z], z_recv.at[z], me.at(z))
        sums = [sums[j] + deep[z, j].astype(F32) for j in range(2)]
    for j in range(2):
        total[j] = sums[j].astype(BF16)
    outs = (dk_ref, dv_ref)
    for d in range(1, 8):
        peer = (head + d) % 8
        for j in range(2):
            send(
                total.at[j, head_rows(peer), :], outs[j].at[:, head_columns(head)],
                head_send.at[j, d], head_recv.at[j, d], own, peer,
            )
    for j in range(2):
        outs[j][:, head_columns(head)] = total[j, head_rows(head), :]
    for d in range(1, 8):
        peer = (head + 8 - d) % 8
        for j in range(2):
            here = outs[j].at[:, head_columns(peer)]
            copy_to(here, here, head_send.at[j, d], head_recv.at[j, d], own, peer).wait_recv()
    for copy in sent:
        copy.wait_send()


def scatter(parts):
    vmem = pl.BlockSpec(memory_space=pltpu.VMEM)
    dma = pltpu.SemaphoreType.DMA
    chunk = (2 * BLOCK, WIDTH)
    out = jax.ShapeDtypeStruct((16, 8 * WIDTH), BF16)
    return pl.pallas_call(
        scatter_kernel,
        out_shape=(out, out),
        in_specs=[vmem],
        out_specs=(vmem, vmem),
        scratch_shapes=[
            pltpu.VMEM((4, 4, 2) + chunk, BF16),
            pltpu.VMEM((2, 4) + chunk, BF16),
            pltpu.VMEM((2, 4, 2) + chunk, BF16),
            pltpu.VMEM((4, 2) + chunk, BF16),
            pltpu.VMEM((4, 2) + chunk, BF16),
            pltpu.VMEM((2, 4, 2) + chunk, BF16),
            pltpu.VMEM((3, 2) + chunk, BF16),
            pltpu.VMEM((2,) + chunk, BF16),
            dma((4, 4)), dma((4, 4)), dma((2, 4)), dma((2, 4)), dma((2, 4)), dma((2, 4)),
            dma((3,)), dma((4,)), dma((2, 8)), dma((2, 8)),
        ],
        compiler_params=pltpu.CompilerParams(
            collective_id=1, has_side_effects=True, vmem_limit_bytes=32 * 2**20
        ),
        name="scatter",
    )(parts)


def body(queries, key_matrix, value_matrix, output, grad_out, log_norm, doc_ids, block_order):
    span = lax.axis_index("blk").astype(jnp.int32).reshape(1)
    kv = gather(key_matrix, value_matrix)
    grad_query, grad_kv = attend(
        span, block_order, doc_ids.reshape(-1, WIDTH), queries, output, grad_out, log_norm, kv, BF16
    )
    return (grad_query,) + tuple(scatter(grad_kv))


def solution(mesh):
    placed = (
        P("blk", "head"),
        P(("blk", "head"), None),
        P(("blk", "head"), None),
        P("blk", "head"),
        P("blk", "head"),
        P("blk", "head"),
        P(),
        P(),
    )
    return jax.shard_map(
        body,
        mesh=mesh,
        in_specs=placed,
        out_specs=(P("blk", "head"), P(("blk", "head"), None), P(("blk", "head"), None)),
        check_vma=False,
    )
```

```python
import functools
import math

import jax
import jax.numpy as jnp
from jax import lax
from jax.experimental import pallas as pl
from jax.experimental.pallas import tpu as pltpu
from jax.sharding import PartitionSpec as P

WIDTH = 128
BLOCK = 64
DOCS = 6
TILE = 256
MASKED = -(2.0**17)
ROOT = math.sqrt(WIDTH)
SCALE = 1.0 / ROOT
EXP2_SCALE = SCALE * math.log2(math.e)
BF16 = jnp.bfloat16
F32 = jnp.float32


def root_parts():
    parts, rest = [], ROOT
    for _ in range(3):
        term = _to_bf16(rest)
        parts.append(term)
        rest -= term
    return parts


def _to_bf16(value):
    mantissa, exponent = math.frexp(value)
    return math.ldexp(round(mantissa * 256), exponent - 8)


ROOT_PARTS = root_parts()


class Place:
    def __init__(self):
        self.span = lax.axis_index("blk")
        self.head = lax.axis_index("head")
        self.core = self.span % 2
        self.x = (self.span // 2) % 4
        self.z = self.span // 8
        self.near_z = (1 + self.z % 2, (2 + 3 * self.z) % 5, 3 * (1 - self.z // 2))

    def at(self, z, dx=0, other=False):
        core = 1 - self.core if other else self.core
        return (z * 4 + (self.x + dx) % 4) * 2 + core

    @property
    def sibling(self):
        return self.at(self.z, 0, True)


def meet(place):
    barrier = pltpu.get_barrier_semaphore()
    peers = [(place.span, (place.head + d) % 8) for d in range(1, 8)]
    peers += [(place.at(z), place.head) for z in place.near_z]
    peers += [(place.at(place.z, 1), place.head), (place.at(place.z, 3), place.head)]
    peers += [(place.sibling, place.head)]
    for peer in peers:
        pl.semaphore_signal(
            barrier, inc=1, device_id=peer, device_id_type=pl.DeviceIdType.MESH
        )
    pl.semaphore_wait(barrier, len(peers))


class Sent:
    def __init__(self, ref):
        self.ref = ref

    @property
    def at(self):
        return self

    def __getitem__(self, index):
        return (self.ref, index)


def copy_to(src, dst, send, recv, span, head):
    ref, index = send
    send = ref.at[index]
    return pltpu.make_async_remote_copy(
        src_ref=src, dst_ref=dst, send_sem=send, recv_sem=recv,
        device_id=(span, head), device_id_type=pl.DeviceIdType.MESH,
    )


def head_rows(head):
    return pl.ds(pl.multiple_of(head * 16, 16), 16)


def head_columns(head):
    return pl.ds(pl.multiple_of(head * WIDTH, WIDTH), WIDTH)


OWN, LEFT, RIGHT, FAR = 0, 3, 1, 2
UNITS = [
    (0, OWN), (1, OWN), (0, LEFT), (0, RIGHT), (2, OWN), (0, FAR), (1, LEFT), (1, RIGHT),
    (3, OWN), (1, FAR), (2, LEFT), (2, RIGHT), (2, FAR), (3, LEFT), (3, RIGHT), (3, FAR),
]
STEP_OF = {unit: step for step, unit in enumerate(UNITS)}


def backward_kernel(
    order_ref, docs_hbm, q_hbm, o_hbm, g_hbm, norm_ref, k_hbm, v_hbm,
    dq_ref, dk_ref, dv_ref,
    docs_ref, q_ref, o_ref, g_ref, k_ref, v_ref,
    kv_ref, q_all, g_all, q_turn, g_turn, dq_turn, work,
    part, sib_out, sib, far, near, deep, far_out, near_out, deep_out, total,
    load_sem,
    head_send, head_recv, z_send, z_recv, x_send, x_recv, f_send, f_recv, s_send, s_recv,
    p_send, p_recv, rf_send, rf_recv, rx_send, rx_recv, rz_send, rz_recv, rh_send, rh_recv,
):
    (
        head_send, z_send, x_send, f_send, s_send, p_send, rf_send, rx_send, rz_send, rh_send
    ) = map(
        Sent,
        (head_send, z_send, x_send, f_send, s_send, p_send, rf_send, rx_send, rz_send, rh_send),
    )
    me = Place()
    own, head = me.span, me.head
    order = (me.z,) + me.near_z
    left, right, sibling = me.at(me.z, LEFT), me.at(me.z, RIGHT), me.sibling

    loads = [
        pltpu.make_async_copy(src, dst, load_sem.at[i])
        for i, (src, dst) in enumerate(
            (
                (k_hbm, k_ref), (v_hbm, v_ref), (q_hbm, q_ref), (g_hbm, g_ref),
                (o_hbm, o_ref), (docs_hbm, docs_ref),
            )
        )
    ]
    for load in loads:
        load.start()
    meet(me)
    loads[0].wait()
    loads[1].wait()

    sent = []

    def send(src, dst, sent_sem, recv_sem, span, to_head):
        copy_to(src, dst, sent_sem, recv_sem, span, to_head).start()
        sent.append((src.shape, sent_sem))

    def arrived(block, recv, span):
        copy_to(block, block, s_send.at[0, 0], recv, span, head).wait_recv()

    for d in range(1, 8):
        peer = (head + d) % 8
        for j, ref in enumerate((k_ref, v_ref)):
            send(
                ref.at[:, head_columns(peer)], kv_ref.at[own, j, head_rows(head), :],
                head_send.at[j, d], head_recv.at[j, d], own, peer,
            )
    for j, ref in enumerate((k_ref, v_ref)):
        kv_ref[own, j, head_rows(head), :] = ref[:, head_columns(head)]

    for load in loads[2:]:
        load.wait()
    docs = docs_ref[...]
    starts = [jnp.sum((docs < d).astype(jnp.int32)) for d in range(1, DOCS)]
    lane = lax.broadcasted_iota(jnp.int32, (BLOCK, WIDTH), 1)
    row = lax.broadcasted_iota(jnp.int32, (BLOCK, WIDTH), 0)
    one_hot = (lane == row).astype(F32)
    norm_lane = (lane >= BLOCK) & (lane < BLOCK + 3)
    lanes = lax.broadcasted_iota(jnp.int32, (1, WIDTH), 1)
    norms = norm_ref[...].astype(F32).T
    query_pos, query_start = [], []
    for half in range(2):
        here = slice(half * BLOCK, (half + 1) * BLOCK)
        for h in range(8):
            cols = slice(h * WIDTH, (h + 1) * WIDTH)
            there = slice(h * BLOCK, (h + 1) * BLOCK)
            g = g_ref[here, cols]
            q_all[half, there, :WIDTH] = q_ref[here, cols]
            g_all[half, there, :WIDTH] = g
            norm = norms[here, h : h + 1]
            q_all[half, there, WIDTH:] = jnp.where(norm_lane, norm, one_hot).astype(BF16)
            delta = jnp.sum(g.astype(F32) * o_ref[here, cols].astype(F32), axis=1, keepdims=True)
            high = delta.astype(BF16).astype(F32)
            mid = (delta - high).astype(BF16).astype(F32)
            low = delta - high - mid
            extra = jnp.where(
                lane == 0, high, jnp.where(lane == 1, mid, jnp.where(lane == 2, low, 0.0))
            )
            g_all[half, there, WIDTH:] = extra.astype(BF16)
        q_turn[half] = q_all[half].T
        g_turn[half] = g_all[half].T
        dq_turn[half] = jnp.zeros((WIDTH, 8 * BLOCK), F32)
        pos = lanes + order_ref[2 * own + half] * BLOCK
        start = jnp.zeros_like(pos)
        for s in starts:
            start = jnp.maximum(start, jnp.where(s <= pos, s, 0))
        query_pos.append(jnp.where(lanes < BLOCK, pos, 1 << 20))
        query_start.append(jnp.where(lanes < BLOCK, start, 0))
    tile_lane = lax.broadcasted_iota(jnp.int32, (TILE, WIDTH), 1)
    value_extra = jnp.where(tile_lane < 3, -1.0, 0.0).astype(BF16)
    norm_extra = jnp.zeros((1, WIDTH), F32)
    for i, term in enumerate(ROOT_PARTS):
        norm_extra = jnp.where(lanes == BLOCK + i, -term, norm_extra)

    for d in range(1, 8):
        peer = (head + 8 - d) % 8
        for j in range(2):
            here = kv_ref.at[own, j, head_rows(peer), :]
            copy_to(here, here, head_send.at[j, d], head_recv.at[j, d], own, peer).wait_recv()

    def over(block, k, which):
        send(block, block, s_send.at[k, which], s_recv.at[k, which], sibling, head)

    def give_column(k):
        span = me.at(order[k])
        block = kv_ref.at[span]
        if k > 0:
            arrived(block, z_recv.at[order[k]], span)
        send(block, block, x_send.at[0, k], x_recv.at[0, k], right, head)
        send(block, block, x_send.at[1, k], x_recv.at[1, k], left, head)
        if k == 0:
            for i, z in enumerate(me.near_z):
                send(block, block, z_send.at[i], z_recv.at[me.z], me.at(z), head)
        over(block, k, 0)

    def give_beside(k):
        block = kv_ref.at[me.at(order[k], LEFT)]
        arrived(block, x_recv.at[0, k], left)
        send(block.at[0], block.at[0], f_send.at[0, k], f_recv.at[0, k], right, head)
        over(block, k, 1)
        block = kv_ref.at[me.at(order[k], RIGHT)]
        arrived(block, x_recv.at[1, k], right)
        send(block.at[1], block.at[1], f_send.at[1, k], f_recv.at[1, k], left, head)
        over(block, k, 2)

    def give_far(k):
        block = kv_ref.at[me.at(order[k], FAR)]
        arrived(block.at[0], f_recv.at[0, k], left)
        over(block.at[0], k, 3)
        arrived(block.at[1], f_recv.at[1, k], right)
        over(block.at[1], k, 4)

    def ready(k, dx):
        block = kv_ref.at[me.at(order[k], dx, True)]
        if dx == FAR:
            arrived(block.at[0], s_recv.at[k, 3], sibling)
            arrived(block.at[1], s_recv.at[k, 4], sibling)
        else:
            arrived(block, s_recv.at[k, {OWN: 0, LEFT: 1, RIGHT: 2}[dx]], sibling)

    def pair(k, dx, j):
        step = STEP_OF[k, dx]
        return part[step, j] + sib[step, j].astype(F32)

    def met(k, dx):
        step = STEP_OF[k, dx]
        arrived(sib.at[step], p_recv.at[step], sibling)

    def sum_far(k):
        met(k, FAR)
        for j, span in enumerate((right, left)):
            far_out[k, j] = pair(k, FAR, j).astype(BF16)
            send(far_out.at[k, j], far.at[j, k], rf_send.at[j, k], rf_recv.at[j, k], span, head)

    def sum_beside(k):
        for i, (dx, span, source) in enumerate(((RIGHT, right, left), (LEFT, left, right))):
            met(k, dx)
            arrived(far.at[i, k], rf_recv.at[i, k], source)
            near_out[i, k, i] = (pair(k, dx, i) + far[i, k].astype(F32)).astype(BF16)
            near_out[i, k, 1 - i] = pair(k, dx, 1 - i).astype(BF16)
            send(
                near_out.at[i, k], near.at[i, k], rx_send.at[i, k], rx_recv.at[i, k], span, head
            )

    def sum_column(k):
        met(k, OWN)
        arrived(near.at[0, k], rx_recv.at[0, k], left)
        arrived(near.at[1, k], rx_recv.at[1, k], right)
        sums = [
            pair(k, OWN, j) + near[0, k, j].astype(F32) + near[1, k, j].astype(F32)
            for j in range(2)
        ]
        if k == 0:
            return sums
        for j in range(2):
            deep_out[k, j] = sums[j].astype(BF16)
        send(
            deep_out.at[k], deep.at[me.z], rz_send.at[k], rz_recv.at[me.z], me.at(order[k]), head
        )

    before = {
        0: [(give_column, 0)],
        1: [(give_beside, 0), (give_column, 1)],
        2: [(give_column, 2)],
        3: [(give_far, 0)],
        4: [(give_beside, 1), (give_column, 3)],
        6: [(give_beside, 2), (give_far, 1)],
        8: [(give_beside, 3), (give_far, 2)],
        9: [(sum_far, 0)],
        11: [(give_far, 3)],
        13: [(sum_far, 1), (sum_beside, 0)],
        15: [(sum_far, 2)],
    }
    chips = [order[k] * 4 + (me.x + dx) % 4 for k, dx in UNITS]
    block_row = lax.broadcasted_iota(jnp.int32, (BLOCK, WIDTH), 0)

    def unit(step, carry):
        for at, (k, dx) in enumerate(UNITS):

            @pl.when(step == at)
            def _():
                for action, which in before.get(at, []):
                    action(which)
                ready(k, dx)

        chip = chips[0]
        for at in range(1, len(UNITS)):
            chip = jnp.where(step == at, chips[at], chip)
        keys = kv_ref[pl.ds(2 * chip, 2), 0].reshape(TILE, WIDTH)
        values = kv_ref[pl.ds(2 * chip, 2), 1].reshape(TILE, WIDTH)
        key_pos = jnp.concatenate(
            [block_row + order_ref[4 * chip + i] * BLOCK for i in range(4)], axis=0
        )
        value_side = jnp.concatenate([values, value_extra], axis=1)
        keys_turn = keys.T
        grad_keys = grad_values = None
        for half in range(2):
            hidden = (key_pos > query_pos[half]) | (key_pos < query_start[half])
            extra = jnp.where(hidden, MASKED, norm_extra).astype(BF16)
            scores = jnp.dot(
                jnp.concatenate([keys, extra], axis=1), q_turn[half], preferred_element_type=F32
            )
            weights = jnp.exp2(scores * EXP2_SCALE)
            grad_weights = jnp.dot(value_side, g_turn[half], preferred_element_type=F32)
            grad_scores = (weights * grad_weights).astype(BF16)
            to_values = jnp.dot(
                weights.astype(BF16), g_all[half, :, :WIDTH], preferred_element_type=F32
            )
            to_keys = jnp.dot(grad_scores, q_all[half, :, :WIDTH], preferred_element_type=F32)
            dq_turn[half] += jnp.dot(keys_turn, grad_scores, preferred_element_type=F32)
            grad_keys = to_keys if half == 0 else grad_keys + to_keys
            grad_values = to_values if half == 0 else grad_values + to_values
        for i in range(2):
            rows = slice(2 * i * BLOCK, 2 * (i + 1) * BLOCK)
            work[i, 0] = grad_keys[rows] * SCALE
            work[i, 1] = grad_values[rows]
        part[step] = work[me.core]
        sib_out[step] = work[1 - me.core].astype(BF16)
        copy_to(
            sib_out.at[step], sib.at[step], p_send.at[step], p_recv.at[step], sibling, head
        ).start()
        return carry

    lax.fori_loop(0, len(UNITS), unit, 0)
    sum_beside(1)
    sum_far(3)
    for half in range(2):
        dq = (dq_turn[half] * SCALE).T
        for h in range(8):
            dq_ref[half * BLOCK : (half + 1) * BLOCK, h * WIDTH : (h + 1) * WIDTH] = dq[
                h * BLOCK : (h + 1) * BLOCK
            ].astype(BF16)
    sum_beside(2)
    sum_column(1)
    sum_beside(3)
    sum_column(2)
    sum_column(3)
    sums = sum_column(0)
    for z in me.near_z:
        arrived(deep.at[z], rz_recv.at[z], me.at(z))
        sums = [sums[j] + deep[z, j].astype(F32) for j in range(2)]
    for j in range(2):
        total[j] = sums[j].astype(BF16)
    outs = (dk_ref, dv_ref)
    for d in range(1, 8):
        peer = (head + d) % 8
        for j in range(2):
            send(
                total.at[j, head_rows(peer), :], outs[j].at[:, head_columns(head)],
                rh_send.at[j, d], rh_recv.at[j, d], own, peer,
            )
    for j in range(2):
        outs[j][:, head_columns(head)] = total[j, head_rows(head), :]
    for d in range(1, 8):
        peer = (head + 8 - d) % 8
        for j in range(2):
            here = outs[j].at[:, head_columns(peer)]
            copy_to(here, here, rh_send.at[j, d], rh_recv.at[j, d], own, peer).wait_recv()
    sent += [(sib_out.shape[1:], p_send.at[step]) for step in range(len(UNITS))]
    shapes = {
        (2, 2 * BLOCK, WIDTH): kv_ref.at[0],
        (2 * BLOCK, WIDTH): kv_ref.at[0, 0],
        (16, WIDTH): kv_ref.at[0, 0, pl.ds(0, 16), :],
    }
    for shape, sent_sem in sent:
        block = shapes[tuple(shape)]
        copy_to(block, block, sent_sem, s_recv.at[0, 0], sibling, head).wait_send()


def backward(order, docs, queries, output, grad_out, norm_turn, key_matrix, value_matrix):
    smem = pl.BlockSpec(memory_space=pltpu.SMEM)
    vmem = pl.BlockSpec(memory_space=pltpu.VMEM)
    hbm = pl.BlockSpec(memory_space=pl.ANY)
    dma = pltpu.SemaphoreType.DMA
    chunk = (2 * BLOCK, WIDTH)
    rows = 8 * BLOCK
    out = jax.ShapeDtypeStruct(key_matrix.shape, BF16)
    return pl.pallas_call(
        backward_kernel,
        out_shape=(jax.ShapeDtypeStruct(queries.shape, BF16), out, out),
        in_specs=[smem, hbm, hbm, hbm, hbm, vmem, hbm, hbm],
        out_specs=(vmem, vmem, vmem),
        scratch_shapes=[
            pltpu.VMEM(docs.shape, jnp.int32),
            pltpu.VMEM(queries.shape, BF16),
            pltpu.VMEM(queries.shape, BF16),
            pltpu.VMEM(queries.shape, BF16),
            pltpu.VMEM(key_matrix.shape, BF16),
            pltpu.VMEM(key_matrix.shape, BF16),
            pltpu.VMEM((32, 2) + chunk, BF16),
            pltpu.VMEM((2, rows, 2 * WIDTH), BF16),
            pltpu.VMEM((2, rows, 2 * WIDTH), BF16),
            pltpu.VMEM((2, 2 * WIDTH, rows), BF16),
            pltpu.VMEM((2, 2 * WIDTH, rows), BF16),
            pltpu.VMEM((2, WIDTH, rows), F32),
            pltpu.VMEM((2, 2) + chunk, F32),
            pltpu.VMEM((16, 2) + chunk, F32),
            pltpu.VMEM((16, 2) + chunk, BF16),
            pltpu.VMEM((16, 2) + chunk, BF16),
            pltpu.VMEM((2, 4) + chunk, BF16),
            pltpu.VMEM((2, 4, 2) + chunk, BF16),
            pltpu.VMEM((4, 2) + chunk, BF16),
            pltpu.VMEM((4, 2) + chunk, BF16),
            pltpu.VMEM((2, 4, 2) + chunk, BF16),
            pltpu.VMEM((4, 2) + chunk, BF16),
            pltpu.VMEM((2,) + chunk, BF16),
            dma((6,)),
            dma((2, 8)), dma((2, 8)), dma((3,)), dma((4,)), dma((2, 4)), dma((2, 4)),
            dma((2, 4)), dma((2, 4)), dma((4, 5)), dma((4, 5)),
            dma((16,)), dma((16,)), dma((2, 4)), dma((2, 4)), dma((2, 4)), dma((2, 4)),
            dma((4,)), dma((4,)), dma((2, 8)), dma((2, 8)),
        ],
        compiler_params=pltpu.CompilerParams(
            collective_id=0, has_side_effects=True, vmem_limit_bytes=56 * 2**20
        ),
        name="backward",
    )(order, docs, queries, output, grad_out, norm_turn, key_matrix, value_matrix)


def body(queries, key_matrix, value_matrix, output, grad_out, log_norm, doc_ids, block_order):
    return backward(
        block_order, doc_ids.reshape(-1, WIDTH), queries, output, grad_out, log_norm.T,
        key_matrix, value_matrix,
    )


def solution(mesh):
    placed = (
        P("blk", "head"),
        P(("blk", "head"), None),
        P(("blk", "head"), None),
        P("blk", "head"),
        P("blk", "head"),
        P("blk", "head"),
        P(),
        P(),
    )
    return jax.shard_map(
        body,
        mesh=mesh,
        in_specs=placed,
        out_specs=(P("blk", "head"), P(("blk", "head"), None), P(("blk", "head"), None)),
        check_vma=False,
    )
```

```python
import functools
import math

import jax
import jax.numpy as jnp
from jax import lax
from jax.experimental import pallas as pl
from jax.experimental.pallas import tpu as pltpu
from jax.sharding import PartitionSpec as P

WIDTH = 128
BLOCK = 64
DOCS = 6
TILE = 256
MASKED = -(2.0**17)
ROOT = math.sqrt(WIDTH)
SCALE = 1.0 / ROOT
EXP2_SCALE = SCALE * math.log2(math.e)
BF16 = jnp.bfloat16
F32 = jnp.float32


def root_parts():
    parts, rest = [], ROOT
    for _ in range(3):
        term = _to_bf16(rest)
        parts.append(term)
        rest -= term
    return parts


def _to_bf16(value):
    mantissa, exponent = math.frexp(value)
    return math.ldexp(round(mantissa * 256), exponent - 8)


ROOT_PARTS = root_parts()


class Place:
    def __init__(self):
        self.span = lax.axis_index("blk")
        self.head = lax.axis_index("head")
        self.core = self.span % 2
        self.x = (self.span // 2) % 4
        self.z = self.span // 8
        self.high, self.y = self.head // 4, self.head % 4
        self.partner = (1 - self.high) * 4 + self.y
        self.near_z = (1 + self.z % 2, (2 + 3 * self.z) % 5, 3 * (1 - self.z // 2))

    def at(self, z, dx=0, other=False):
        core = 1 - self.core if other else self.core
        return (z * 4 + (self.x + dx) % 4) * 2 + core

    def beside_y(self, d):
        return self.high * 4 + (self.y + d) % 4

    @property
    def sibling(self):
        return self.at(self.z, 0, True)


def meet(place):
    barrier = pltpu.get_barrier_semaphore()
    peers = [(place.span, place.beside_y(d)) for d in range(1, 4)]
    peers += [(place.at(z), place.head) for z in place.near_z]
    peers += [(place.at(z), place.partner) for z in (place.z,) + place.near_z]
    peers += [(place.at(place.z, 1), place.head), (place.at(place.z, 3), place.head)]
    peers += [(place.sibling, place.head)]
    for peer in peers:
        pl.semaphore_signal(
            barrier, inc=1, device_id=peer, device_id_type=pl.DeviceIdType.MESH
        )
    pl.semaphore_wait(barrier, len(peers))


class Sent:
    def __init__(self, ref):
        self.ref = ref

    @property
    def at(self):
        return self

    def __getitem__(self, index):
        return (self.ref, index)


def copy_to(src, dst, send, recv, span, head):
    ref, index = send
    send = ref.at[index]
    return pltpu.make_async_remote_copy(
        src_ref=src, dst_ref=dst, send_sem=send, recv_sem=recv,
        device_id=(span, head), device_id_type=pl.DeviceIdType.MESH,
    )


def head_rows(head):
    return pl.ds(pl.multiple_of(head * 16, 16), 16)


def half_rows(high):
    return pl.ds(pl.multiple_of(high * BLOCK, BLOCK), BLOCK)


def head_columns(head):
    return pl.ds(pl.multiple_of(head * WIDTH, WIDTH), WIDTH)


OWN, LEFT, RIGHT, FAR = 0, 3, 1, 2
UNITS = [
    (0, OWN), (1, OWN), (0, LEFT), (0, RIGHT), (2, OWN), (0, FAR), (1, LEFT), (1, RIGHT),
    (1, FAR), (2, LEFT), (2, RIGHT), (2, FAR), (3, FAR), (3, LEFT), (3, RIGHT), (3, OWN),
]
ALL, MINE, OTHER = 0, 1, 2
ITEMS = [(0, MINE), (1, ALL), (0, OTHER), (2, ALL), (3, ALL)]
STEP_OF = {unit: step for step, unit in enumerate(UNITS)}


def backward_kernel(
    order_ref, docs_hbm, q_hbm, o_hbm, g_hbm, norm_ref, k_hbm, v_hbm,
    dq_ref, dk_ref, dv_ref,
    docs_ref, q_ref, o_ref, g_ref, k_ref, v_ref,
    kv_ref, other_ref, q_all, g_all, q_turn, g_turn, dq_turn, work,
    part, sib_out, sib, far, near, deep, far_out, near_out, deep_out, total, deep_sum, mine_sum,
    load_sem,
    head_send, head_recv, z_send, z_recv, x_send, x_recv, f_send, f_recv, s_send, s_recv,
    p_send, p_recv, rf_send, rf_recv, rx_send, rx_recv, rz_send, rz_recv, rh_send, rh_recv,
):
    (
        head_send, z_send, x_send, f_send, s_send, p_send, rf_send, rx_send, rz_send, rh_send
    ) = map(
        Sent,
        (head_send, z_send, x_send, f_send, s_send, p_send, rf_send, rx_send, rz_send, rh_send),
    )
    me = Place()
    own, head = me.span, me.head
    order = (me.z,) + me.near_z
    left, right, sibling = me.at(me.z, LEFT), me.at(me.z, RIGHT), me.sibling

    loads = [
        pltpu.make_async_copy(src, dst, load_sem.at[i])
        for i, (src, dst) in enumerate(
            (
                (k_hbm, k_ref), (v_hbm, v_ref), (q_hbm, q_ref), (g_hbm, g_ref),
                (o_hbm, o_ref), (docs_hbm, docs_ref),
            )
        )
    ]
    for load in loads:
        load.start()
    meet(me)
    loads[0].wait()
    loads[1].wait()

    sent = []

    def send(src, dst, sent_sem, recv_sem, span, to_head):
        copy_to(src, dst, sent_sem, recv_sem, span, to_head).start()
        sent.append((src.shape, sent_sem))

    def arrived(block, recv, span):
        copy_to(block, block, s_send.at[0, 0], recv, span, head).wait_recv()

    homes = (kv_ref.at[own, :, half_rows(me.high), :], other_ref)
    groups = (me.high, 1 - me.high)
    for d in range(1, 4):
        to = me.beside_y(d)
        for i, (home, group) in enumerate(zip(homes, groups)):
            columns = head_columns(group * 4 + (me.y + d) % 4)
            for j, ref in enumerate((k_ref, v_ref)):
                send(
                    ref.at[:, columns], home.at[j, head_rows(me.y), :],
                    head_send.at[i, j, d], head_recv.at[i, j, d], own, to,
                )
    for j, ref in enumerate((k_ref, v_ref)):
        kv_ref[own, j, head_rows(head), :] = ref[:, head_columns(head)]
        other_ref[j, head_rows(me.y), :] = ref[:, head_columns(me.partner)]

    for load in loads[2:]:
        load.wait()
    docs = docs_ref[...]
    starts = [jnp.sum((docs < d).astype(jnp.int32)) for d in range(1, DOCS)]
    lane = lax.broadcasted_iota(jnp.int32, (BLOCK, WIDTH), 1)
    row = lax.broadcasted_iota(jnp.int32, (BLOCK, WIDTH), 0)
    one_hot = (lane == row).astype(F32)
    norm_lane = (lane >= BLOCK) & (lane < BLOCK + 3)
    lanes = lax.broadcasted_iota(jnp.int32, (1, WIDTH), 1)
    norms = norm_ref[...].astype(F32).T
    query_pos, query_start = [], []

    def prepare(half):
        here = slice(half * BLOCK, (half + 1) * BLOCK)
        for h in range(8):
            cols = slice(h * WIDTH, (h + 1) * WIDTH)
            there = slice(h * BLOCK, (h + 1) * BLOCK)
            g = g_ref[here, cols]
            q_all[half, there, :WIDTH] = q_ref[here, cols]
            g_all[half, there, :WIDTH] = g
            norm = norms[here, h : h + 1]
            q_all[half, there, WIDTH:] = jnp.where(norm_lane, norm, one_hot).astype(BF16)
            delta = jnp.sum(g.astype(F32) * o_ref[here, cols].astype(F32), axis=1, keepdims=True)
            high = delta.astype(BF16).astype(F32)
            mid = (delta - high).astype(BF16).astype(F32)
            low = delta - high - mid
            extra = jnp.where(
                lane == 0, high, jnp.where(lane == 1, mid, jnp.where(lane == 2, low, 0.0))
            )
            g_all[half, there, WIDTH:] = extra.astype(BF16)
        q_turn[half] = q_all[half].T
        g_turn[half] = g_all[half].T
        dq_turn[half] = jnp.zeros((WIDTH, 8 * BLOCK), F32)
        pos = lanes + order_ref[2 * own + half] * BLOCK
        start = jnp.zeros_like(pos)
        for s in starts:
            start = jnp.maximum(start, jnp.where(s <= pos, s, 0))
        query_pos.append(jnp.where(lanes < BLOCK, pos, 1 << 20))
        query_start.append(jnp.where(lanes < BLOCK, start, 0))

    prepare(0)
    tile_lane = lax.broadcasted_iota(jnp.int32, (TILE, WIDTH), 1)
    value_extra = jnp.where(tile_lane < 3, -1.0, 0.0).astype(BF16)
    norm_extra = jnp.zeros((1, WIDTH), F32)
    for i, term in enumerate(ROOT_PARTS):
        norm_extra = jnp.where(lanes == BLOCK + i, -term, norm_extra)

    for d in range(1, 4):
        source = me.beside_y(4 - d)
        for i, home in enumerate(homes):
            for j in range(2):
                here = home.at[j, head_rows((me.y + 4 - d) % 4), :]
                copy_to(
                    here, here, head_send.at[i, j, d], head_recv.at[i, j, d], own, source
                ).wait_recv()

    for i, z in enumerate(me.near_z):
        send(homes[0], homes[0], z_send.at[0, i], z_recv.at[me.high, me.z], me.at(z), head)
    for i, z in enumerate((me.z,) + me.near_z):
        send(other_ref, homes[0], z_send.at[1, i], z_recv.at[me.high, me.z], me.at(z), me.partner)

    def item(i, dx, other=False):
        k, which = ITEMS[i]
        block = kv_ref.at[me.at(order[k], dx, other)]
        if which == ALL:
            return block
        return block.at[:, half_rows(me.high if which == MINE else 1 - me.high), :]

    def over(block, i, which):
        send(block, block, s_send.at[i, which], s_recv.at[i, which], sibling, head)

    def give_column(i):
        k, which = ITEMS[i]
        span = me.at(order[k])
        for high in (me.high, 1 - me.high):
            if which == ALL or (which == OTHER and high is not me.high):
                half = kv_ref.at[span, :, half_rows(high), :]
                arrived(half, z_recv.at[high, order[k]], span)
        block = item(i, OWN)
        send(block, block, x_send.at[0, i], x_recv.at[0, i], right, head)
        send(block, block, x_send.at[1, i], x_recv.at[1, i], left, head)
        over(block, i, 0)

    def give_beside(i):
        block = item(i, LEFT)
        arrived(block, x_recv.at[0, i], left)
        send(block.at[0], block.at[0], f_send.at[0, i], f_recv.at[0, i], right, head)
        over(block, i, 1)
        block = item(i, RIGHT)
        arrived(block, x_recv.at[1, i], right)
        send(block.at[1], block.at[1], f_send.at[1, i], f_recv.at[1, i], left, head)
        over(block, i, 2)

    def give_far(i):
        block = item(i, FAR)
        arrived(block.at[0], f_recv.at[0, i], left)
        over(block.at[0], i, 3)
        arrived(block.at[1], f_recv.at[1, i], right)
        over(block.at[1], i, 4)

    def ready(k, dx):
        for i, (at, _) in enumerate(ITEMS):
            if at != k:
                continue
            block = item(i, dx, True)
            if dx == FAR:
                arrived(block.at[0], s_recv.at[i, 3], sibling)
                arrived(block.at[1], s_recv.at[i, 4], sibling)
            else:
                arrived(block, s_recv.at[i, {OWN: 0, LEFT: 1, RIGHT: 2}[dx]], sibling)

    def pair(k, dx, j):
        step = STEP_OF[k, dx]
        return part[step, j] + sib[step, j].astype(F32)

    def met(k, dx):
        step = STEP_OF[k, dx]
        arrived(sib.at[step], p_recv.at[step], sibling)

    def sum_far(k):
        met(k, FAR)
        for j, span in enumerate((right, left)):
            far_out[k, j] = pair(k, FAR, j).astype(BF16)
            send(far_out.at[k, j], far.at[j, k], rf_send.at[j, k], rf_recv.at[j, k], span, head)

    def sum_beside(k):
        for i, (dx, span, source) in enumerate(((RIGHT, right, left), (LEFT, left, right))):
            met(k, dx)
            arrived(far.at[i, k], rf_recv.at[i, k], source)
            near_out[i, k, i] = (pair(k, dx, i) + far[i, k].astype(F32)).astype(BF16)
            near_out[i, k, 1 - i] = pair(k, dx, 1 - i).astype(BF16)
            send(
                near_out.at[i, k], near.at[i, k], rx_send.at[i, k], rx_recv.at[i, k], span, head
            )

    def sum_column(k):
        met(k, OWN)
        arrived(near.at[0, k], rx_recv.at[0, k], left)
        arrived(near.at[1, k], rx_recv.at[1, k], right)
        sums = [
            pair(k, OWN, j) + near[0, k, j].astype(F32) + near[1, k, j].astype(F32)
            for j in range(2)
        ]
        for j in range(2):
            deep_out[k, j] = sums[j].astype(BF16)
        if k == 0:
            for j in range(2):
                deep_sum[j] = sums[j]
                mine_sum[j] = deep_sum[j, half_rows(me.high), :]
        for i, to in enumerate((head, me.partner)):
            if k > 0 or i > 0:
                send(
                    deep_out.at[k, :, half_rows(me.high if i == 0 else 1 - me.high), :],
                    deep.at[me.high, me.z], rz_send.at[i, k], rz_recv.at[me.high, me.z],
                    me.at(order[k]), to,
                )

    before = {
        0: [(give_beside, 0), (give_column, 1), (give_column, 2)],
        1: [(give_column, 3), (give_far, 0)],
        2: [(give_beside, 1), (give_column, 4), (give_beside, 2)],
        3: [(give_far, 1)],
        4: [(give_beside, 3), (give_far, 2)],
        6: [(give_beside, 4), (give_far, 3)],
        8: [(sum_far, 0)],
        9: [(give_far, 4)],
        11: [(sum_far, 1)],
        12: [(sum_beside, 0)],
        14: [(sum_far, 2)],
        15: [(sum_far, 3), (sum_beside, 1)],
    }
    chips = [order[k] * 4 + (me.x + dx) % 4 for k, dx in UNITS]
    give_column(0)
    prepare(1)
    block_row = lax.broadcasted_iota(jnp.int32, (BLOCK, WIDTH), 0)

    def unit(step, carry):
        for at, (k, dx) in enumerate(UNITS):

            @pl.when(step == at)
            def _():
                for action, which in before.get(at, []):
                    action(which)
                ready(k, dx)

        chip = chips[0]
        for at in range(1, len(UNITS)):
            chip = jnp.where(step == at, chips[at], chip)
        keys = kv_ref[pl.ds(2 * chip, 2), 0].reshape(TILE, WIDTH)
        values = kv_ref[pl.ds(2 * chip, 2), 1].reshape(TILE, WIDTH)
        key_pos = jnp.concatenate(
            [block_row + order_ref[4 * chip + i] * BLOCK for i in range(4)], axis=0
        )
        value_side = jnp.concatenate([values, value_extra], axis=1)
        keys_turn = keys.T
        grad_keys = grad_values = None
        for half in range(2):
            hidden = (key_pos > query_pos[half]) | (key_pos < query_start[half])
            extra = jnp.where(hidden, MASKED, norm_extra).astype(BF16)
            scores = jnp.dot(
                jnp.concatenate([keys, extra], axis=1), q_turn[half], preferred_element_type=F32
            )
            weights = jnp.exp2(scores * EXP2_SCALE)
            grad_weights = jnp.dot(value_side, g_turn[half], preferred_element_type=F32)
            grad_scores = (weights * grad_weights).astype(BF16)
            to_values = jnp.dot(
                weights.astype(BF16), g_all[half, :, :WIDTH], preferred_element_type=F32
            )
            to_keys = jnp.dot(grad_scores, q_all[half, :, :WIDTH], preferred_element_type=F32)
            dq_turn[half] += jnp.dot(keys_turn, grad_scores, preferred_element_type=F32)
            grad_keys = to_keys if half == 0 else grad_keys + to_keys
            grad_values = to_values if half == 0 else grad_values + to_values
        for i in range(2):
            rows = slice(2 * i * BLOCK, 2 * (i + 1) * BLOCK)
            work[i, 0] = grad_keys[rows] * SCALE
            work[i, 1] = grad_values[rows]
        part[step] = work[me.core]
        sib_out[step] = work[1 - me.core].astype(BF16)
        copy_to(
            sib_out.at[step], sib.at[step], p_send.at[step], p_recv.at[step], sibling, head
        ).start()
        return carry

    lax.fori_loop(0, len(UNITS), unit, 0)
    sum_beside(2)
    sum_column(0)
    for half in range(2):
        dq = (dq_turn[half] * SCALE).T
        for h in range(8):
            dq_ref[half * BLOCK : (half + 1) * BLOCK, h * WIDTH : (h + 1) * WIDTH] = dq[
                h * BLOCK : (h + 1) * BLOCK
            ].astype(BF16)
    sum_column(1)
    sum_beside(3)
    sum_column(2)
    sum_column(3)
    for i, group in enumerate(groups):
        sums = None if i else [mine_sum[j] for j in range(2)]
        for z in order[1 - i :]:
            arrived(deep.at[group, z], rz_recv.at[group, z], me.at(z))
            got = [deep[group, z, j].astype(F32) for j in range(2)]
            sums = got if sums is None else [sums[j] + got[j] for j in range(2)]
        for j in range(2):
            total[i, j] = sums[j].astype(BF16)
    outs = (dk_ref, dv_ref)
    for d in range(1, 4):
        for i, group in enumerate(groups):
            columns = head_columns(group * 4 + me.y)
            for j in range(2):
                send(
                    total.at[i, j, head_rows((me.y + d) % 4), :], outs[j].at[:, columns],
                    rh_send.at[i, j, d], rh_recv.at[i, j, d], own, me.beside_y(d),
                )
    for i, group in enumerate(groups):
        for j in range(2):
            outs[j][:, head_columns(group * 4 + me.y)] = total[i, j, head_rows(me.y), :]
    for d in range(1, 4):
        for i, group in enumerate(groups):
            for j in range(2):
                here = outs[j].at[:, head_columns(group * 4 + (me.y + 4 - d) % 4)]
                copy_to(
                    here, here, rh_send.at[i, j, d], rh_recv.at[i, j, d], own, me.beside_y(4 - d)
                ).wait_recv()
    sent += [(sib_out.shape[1:], p_send.at[step]) for step in range(len(UNITS))]
    shapes = {
        (2, 2 * BLOCK, WIDTH): kv_ref.at[0],
        (2 * BLOCK, WIDTH): kv_ref.at[0, 0],
        (2, BLOCK, WIDTH): other_ref,
        (BLOCK, WIDTH): other_ref.at[0],
        (16, WIDTH): kv_ref.at[0, 0, pl.ds(0, 16), :],
    }
    for shape, sent_sem in sent:
        block = shapes[tuple(shape)]
        copy_to(block, block, sent_sem, s_recv.at[0, 0], sibling, head).wait_send()


def backward(order, docs, queries, output, grad_out, norm_turn, key_matrix, value_matrix):
    smem = pl.BlockSpec(memory_space=pltpu.SMEM)
    vmem = pl.BlockSpec(memory_space=pltpu.VMEM)
    hbm = pl.BlockSpec(memory_space=pl.ANY)
    dma = pltpu.SemaphoreType.DMA
    chunk = (2 * BLOCK, WIDTH)
    rows = 8 * BLOCK
    out = jax.ShapeDtypeStruct(key_matrix.shape, BF16)
    return pl.pallas_call(
        backward_kernel,
        out_shape=(jax.ShapeDtypeStruct(queries.shape, BF16), out, out),
        in_specs=[smem, hbm, hbm, hbm, hbm, vmem, hbm, hbm],
        out_specs=(vmem, vmem, vmem),
        scratch_shapes=[
            pltpu.VMEM(docs.shape, jnp.int32),
            pltpu.VMEM(queries.shape, BF16),
            pltpu.VMEM(queries.shape, BF16),
            pltpu.VMEM(queries.shape, BF16),
            pltpu.VMEM(key_matrix.shape, BF16),
            pltpu.VMEM(key_matrix.shape, BF16),
            pltpu.VMEM((32, 2) + chunk, BF16),
            pltpu.VMEM((2, BLOCK, WIDTH), BF16),
            pltpu.VMEM((2, rows, 2 * WIDTH), BF16),
            pltpu.VMEM((2, rows, 2 * WIDTH), BF16),
            pltpu.VMEM((2, 2 * WIDTH, rows), BF16),
            pltpu.VMEM((2, 2 * WIDTH, rows), BF16),
            pltpu.VMEM((2, WIDTH, rows), F32),
            pltpu.VMEM((2, 2) + chunk, F32),
            pltpu.VMEM((16, 2) + chunk, F32),
            pltpu.VMEM((16, 2) + chunk, BF16),
            pltpu.VMEM((16, 2) + chunk, BF16),
            pltpu.VMEM((2, 4) + chunk, BF16),
            pltpu.VMEM((2, 4, 2) + chunk, BF16),
            pltpu.VMEM((2, 4, 2, BLOCK, WIDTH), BF16),
            pltpu.VMEM((4, 2) + chunk, BF16),
            pltpu.VMEM((2, 4, 2) + chunk, BF16),
            pltpu.VMEM((4, 2) + chunk, BF16),
            pltpu.VMEM((2, 2, BLOCK, WIDTH), BF16),
            pltpu.VMEM((2,) + chunk, F32),
            pltpu.VMEM((2, BLOCK, WIDTH), F32),
            dma((6,)),
            dma((2, 2, 4)), dma((2, 2, 4)), dma((2, 4)), dma((2, 4)), dma((2, 5)), dma((2, 5)),
            dma((2, 5)), dma((2, 5)), dma((5, 5)), dma((5, 5)),
            dma((16,)), dma((16,)), dma((2, 4)), dma((2, 4)), dma((2, 4)), dma((2, 4)),
            dma((2, 4)), dma((2, 4)), dma((2, 2, 4)), dma((2, 2, 4)),
        ],
        compiler_params=pltpu.CompilerParams(
            collective_id=0, has_side_effects=True, vmem_limit_bytes=56 * 2**20
        ),
        name="backward",
    )(order, docs, queries, output, grad_out, norm_turn, key_matrix, value_matrix)


def body(queries, key_matrix, value_matrix, output, grad_out, log_norm, doc_ids, block_order):
    return backward(
        block_order, doc_ids.reshape(-1, WIDTH), queries, output, grad_out, log_norm.T,
        key_matrix, value_matrix,
    )


def solution(mesh):
    placed = (
        P("blk", "head"),
        P(("blk", "head"), None),
        P(("blk", "head"), None),
        P("blk", "head"),
        P("blk", "head"),
        P("blk", "head"),
        P(),
        P(),
    )
    return jax.shard_map(
        body,
        mesh=mesh,
        in_specs=placed,
        out_specs=(P("blk", "head"), P(("blk", "head"), None), P(("blk", "head"), None)),
        check_vma=False,
    )
```

```python
import functools
import math

import jax
import jax.numpy as jnp
from jax import lax
from jax.experimental import pallas as pl
from jax.experimental.pallas import tpu as pltpu
from jax.sharding import PartitionSpec as P

WIDTH = 128
BLOCK = 64
DOCS = 6
TILE = 256
MASKED = -(2.0**17)
ROOT = math.sqrt(WIDTH)
SCALE = 1.0 / ROOT
EXP2_SCALE = SCALE * math.log2(math.e)
BF16 = jnp.bfloat16
F32 = jnp.float32


def root_parts():
    parts, rest = [], ROOT
    for _ in range(3):
        term = _to_bf16(rest)
        parts.append(term)
        rest -= term
    return parts


def _to_bf16(value):
    mantissa, exponent = math.frexp(value)
    return math.ldexp(round(mantissa * 256), exponent - 8)


ROOT_PARTS = root_parts()


class Place:
    def __init__(self):
        self.span = lax.axis_index("blk")
        self.head = lax.axis_index("head")
        self.core = self.span % 2
        self.x = (self.span // 2) % 4
        self.z = self.span // 8
        self.high, self.y = self.head // 4, self.head % 4
        self.partner = (1 - self.high) * 4 + self.y
        self.near_z = (1 + self.z % 2, (2 + 3 * self.z) % 5, 3 * (1 - self.z // 2))

    def at(self, z, dx=0, other=False):
        core = 1 - self.core if other else self.core
        return (z * 4 + (self.x + dx) % 4) * 2 + core

    def beside_y(self, d):
        return self.high * 4 + (self.y + d) % 4

    @property
    def sibling(self):
        return self.at(self.z, 0, True)


def meet(place):
    barrier = pltpu.get_barrier_semaphore()
    peers = [(place.span, place.beside_y(d)) for d in range(1, 4)]
    peers += [(place.at(z), place.head) for z in place.near_z]
    peers += [(place.at(z), place.partner) for z in (place.z,) + place.near_z]
    peers += [(place.at(place.z, dx), place.head) for dx in (1, 2, 3)]
    peers += [(place.sibling, place.head)]
    for peer in peers:
        pl.semaphore_signal(
            barrier, inc=1, device_id=peer, device_id_type=pl.DeviceIdType.MESH
        )
    pl.semaphore_wait(barrier, len(peers))


class Sent:
    def __init__(self, ref):
        self.ref = ref

    @property
    def at(self):
        return self

    def __getitem__(self, index):
        return (self.ref, index)


def copy_to(src, dst, send, recv, span, head):
    ref, index = send
    send = ref.at[index]
    return pltpu.make_async_remote_copy(
        src_ref=src, dst_ref=dst, send_sem=send, recv_sem=recv,
        device_id=(span, head), device_id_type=pl.DeviceIdType.MESH,
    )


def head_rows(head):
    return pl.ds(pl.multiple_of(head * 16, 16), 16)


def half_rows(high):
    return pl.ds(pl.multiple_of(high * BLOCK, BLOCK), BLOCK)


def head_columns(head):
    return pl.ds(pl.multiple_of(head * WIDTH, WIDTH), WIDTH)


OWN, LEFT, RIGHT, FAR = 0, 3, 1, 2
UNITS = [
    (0, OWN), (1, OWN), (2, OWN), (0, LEFT), (0, RIGHT), (0, FAR), (1, LEFT), (1, RIGHT),
    (1, FAR), (2, LEFT), (2, RIGHT), (2, FAR), (3, LEFT), (3, RIGHT), (3, FAR), (3, OWN),
]
ALL, MINE, OTHER = 0, 1, 2
ITEMS = [(0, MINE), (1, ALL), (0, OTHER), (2, ALL), (3, ALL)]
STEP_OF = {unit: step for step, unit in enumerate(UNITS)}


def backward_kernel(
    order_ref, docs_hbm, q_hbm, o_hbm, g_hbm, norm_ref, k_hbm, v_hbm,
    dq_ref, dk_ref, dv_ref,
    docs_ref, q_ref, o_ref, g_ref, k_ref, v_ref,
    kv_ref, other_ref, q_all, g_all, q_turn, g_turn, dq_turn, work,
    part, sib_out, sib, near, deep, near_out, deep_out, total, deep_sum, mine_sum,
    load_sem,
    head_send, head_recv, z_send, z_recv, x_send, x_recv, s_send, s_recv,
    p_send, p_recv, rx_send, rx_recv, rz_send, rz_recv, rh_send, rh_recv,
):
    head_send, z_send, x_send, s_send, p_send, rx_send, rz_send, rh_send = map(
        Sent, (head_send, z_send, x_send, s_send, p_send, rx_send, rz_send, rh_send)
    )
    me = Place()
    own, head = me.span, me.head
    order = (me.z,) + me.near_z
    sibling = me.sibling

    loads = [
        pltpu.make_async_copy(src, dst, load_sem.at[i])
        for i, (src, dst) in enumerate(
            (
                (k_hbm, k_ref), (v_hbm, v_ref), (q_hbm, q_ref), (g_hbm, g_ref),
                (o_hbm, o_ref), (docs_hbm, docs_ref),
            )
        )
    ]
    for load in loads:
        load.start()
    meet(me)
    loads[0].wait()
    loads[1].wait()

    sent = []

    def send(src, dst, sent_sem, recv_sem, span, to_head):
        copy_to(src, dst, sent_sem, recv_sem, span, to_head).start()
        sent.append((src.shape, sent_sem))

    def arrived(block, recv, span):
        copy_to(block, block, s_send.at[0, 0], recv, span, head).wait_recv()

    homes = (kv_ref.at[own, :, half_rows(me.high), :], other_ref)
    groups = (me.high, 1 - me.high)
    for d in range(1, 4):
        to = me.beside_y(d)
        for i, (home, group) in enumerate(zip(homes, groups)):
            columns = head_columns(group * 4 + (me.y + d) % 4)
            for j, ref in enumerate((k_ref, v_ref)):
                send(
                    ref.at[:, columns], home.at[j, head_rows(me.y), :],
                    head_send.at[i, j, d], head_recv.at[i, j, d], own, to,
                )
    for j, ref in enumerate((k_ref, v_ref)):
        kv_ref[own, j, head_rows(head), :] = ref[:, head_columns(head)]
        other_ref[j, head_rows(me.y), :] = ref[:, head_columns(me.partner)]

    for load in loads[2:]:
        load.wait()
    docs = docs_ref[...]
    starts = [jnp.sum((docs < d).astype(jnp.int32)) for d in range(1, DOCS)]
    lane = lax.broadcasted_iota(jnp.int32, (BLOCK, WIDTH), 1)
    row = lax.broadcasted_iota(jnp.int32, (BLOCK, WIDTH), 0)
    one_hot = (lane == row).astype(F32)
    norm_lane = (lane >= BLOCK) & (lane < BLOCK + 3)
    lanes = lax.broadcasted_iota(jnp.int32, (1, WIDTH), 1)
    norms = norm_ref[...].astype(F32).T
    query_pos, query_start = [], []

    def prepare(half):
        here = slice(half * BLOCK, (half + 1) * BLOCK)
        for h in range(8):
            cols = slice(h * WIDTH, (h + 1) * WIDTH)
            there = slice(h * BLOCK, (h + 1) * BLOCK)
            g = g_ref[here, cols]
            q_all[half, there, :WIDTH] = q_ref[here, cols]
            g_all[half, there, :WIDTH] = g
            norm = norms[here, h : h + 1]
            q_all[half, there, WIDTH:] = jnp.where(norm_lane, norm, one_hot).astype(BF16)
            delta = jnp.sum(g.astype(F32) * o_ref[here, cols].astype(F32), axis=1, keepdims=True)
            high = delta.astype(BF16).astype(F32)
            mid = (delta - high).astype(BF16).astype(F32)
            low = delta - high - mid
            extra = jnp.where(
                lane == 0, high, jnp.where(lane == 1, mid, jnp.where(lane == 2, low, 0.0))
            )
            g_all[half, there, WIDTH:] = extra.astype(BF16)
        q_turn[half] = q_all[half].T
        g_turn[half] = g_all[half].T
        dq_turn[half] = jnp.zeros((WIDTH, 8 * BLOCK), F32)
        pos = lanes + order_ref[2 * own + half] * BLOCK
        start = jnp.zeros_like(pos)
        for s in starts:
            start = jnp.maximum(start, jnp.where(s <= pos, s, 0))
        query_pos.append(jnp.where(lanes < BLOCK, pos, 1 << 20))
        query_start.append(jnp.where(lanes < BLOCK, start, 0))

    prepare(0)
    tile_lane = lax.broadcasted_iota(jnp.int32, (TILE, WIDTH), 1)
    value_extra = jnp.where(tile_lane < 3, -1.0, 0.0).astype(BF16)
    norm_extra = jnp.zeros((1, WIDTH), F32)
    for i, term in enumerate(ROOT_PARTS):
        norm_extra = jnp.where(lanes == BLOCK + i, -term, norm_extra)

    for d in range(1, 4):
        source = me.beside_y(4 - d)
        for i, home in enumerate(homes):
            for j in range(2):
                here = home.at[j, head_rows((me.y + 4 - d) % 4), :]
                copy_to(
                    here, here, head_send.at[i, j, d], head_recv.at[i, j, d], own, source
                ).wait_recv()

    def give_deep(k):
        if k > 0:
            send(
                homes[0], homes[0], z_send.at[0, k], z_recv.at[me.high, me.z],
                me.at(order[k]), head,
            )
        send(
            other_ref, homes[0], z_send.at[1, k], z_recv.at[me.high, me.z],
            me.at(order[k]), me.partner,
        )

    def item(i, dx, other=False):
        k, which = ITEMS[i]
        block = kv_ref.at[me.at(order[k], dx, other)]
        if which == ALL:
            return block
        return block.at[:, half_rows(me.high if which == MINE else 1 - me.high), :]

    def over(block, i, which):
        send(block, block, s_send.at[i, which], s_recv.at[i, which], sibling, head)

    def give_column(i):
        k, which = ITEMS[i]
        span = me.at(order[k])
        for high in (me.high, 1 - me.high):
            if which == ALL or (which == OTHER and high is not me.high):
                half = kv_ref.at[span, :, half_rows(high), :]
                arrived(half, z_recv.at[high, order[k]], span)
        block = item(i, OWN)
        for dx in (FAR, RIGHT, LEFT):
            send(block, block, x_send.at[dx, i], x_recv.at[dx, i], me.at(me.z, dx), head)
        over(block, i, OWN)

    def give_on(i, *steps):
        for dx in steps:
            block = item(i, dx)
            arrived(block, x_recv.at[4 - dx, i], me.at(me.z, dx))
            over(block, i, dx)

    def ready(k, dx):
        for i, (at, _) in enumerate(ITEMS):
            if at != k:
                continue
            arrived(item(i, dx, True), s_recv.at[i, dx], sibling)

    def pair(k, dx, j):
        step = STEP_OF[k, dx]
        return part[step, j] + sib[step, j].astype(F32)

    def met(k, dx):
        step = STEP_OF[k, dx]
        arrived(sib.at[step], p_recv.at[step], sibling)

    def give_sum(step):
        k, dx = UNITS[step]
        met(k, dx)
        for j in range(2):
            near_out[dx, k, j] = pair(k, dx, j).astype(BF16)
        send(
            near_out.at[dx, k], near.at[dx, k], rx_send.at[dx, k], rx_recv.at[dx, k],
            me.at(me.z, dx), head,
        )

    def sum_column(k):
        met(k, OWN)
        sums = [pair(k, OWN, j) for j in range(2)]
        for dx in (LEFT, RIGHT, FAR):
            arrived(near.at[dx, k], rx_recv.at[dx, k], me.at(me.z, 4 - dx))
            sums = [sums[j] + near[dx, k, j].astype(F32) for j in range(2)]
        for j in range(2):
            deep_out[k, j] = sums[j].astype(BF16)
        if k == 0:
            for j in range(2):
                deep_sum[j] = sums[j]
                mine_sum[j] = deep_sum[j, half_rows(me.high), :]
        for i, to in enumerate((head, me.partner)):
            if k > 0 or i > 0:
                send(
                    deep_out.at[k, :, half_rows(me.high if i == 0 else 1 - me.high), :],
                    deep.at[me.high, me.z], rz_send.at[i, k], rz_recv.at[me.high, me.z],
                    me.at(order[k]), to,
                )

    before = {
        0: [(give_column, 1), (give_column, 2)],
        1: [(give_on, 0, LEFT, RIGHT), (give_column, 3)],
        2: [(give_on, 0, FAR), (give_column, 4)],
        3: [(give_on, 2, LEFT, RIGHT), (give_on, 1, LEFT, RIGHT)],
        4: [(give_on, 2, FAR), (give_on, 1, FAR)],
        6: [(give_sum, 3)],
        7: [(give_sum, 4), (give_on, 3, LEFT, RIGHT)],
        8: [(give_sum, 5), (give_on, 3, FAR)],
        9: [(give_sum, 6)],
        10: [(give_sum, 7), (give_on, 4, LEFT, RIGHT)],
        11: [(give_sum, 8), (give_on, 4, FAR)],
        12: [(give_sum, 9)],
        13: [(give_sum, 10)],
        14: [(give_sum, 11), (sum_column, 0)],
        15: [(give_sum, 12)],
    }
    chips = [order[k] * 4 + (me.x + dx) % 4 for k, dx in UNITS]
    give_deep(1)
    give_deep(0)
    give_column(0)
    prepare(1)
    give_deep(2)
    give_deep(3)
    block_row = lax.broadcasted_iota(jnp.int32, (BLOCK, WIDTH), 0)

    def unit(step, carry):
        for at, (k, dx) in enumerate(UNITS):

            @pl.when(step == at)
            def _():
                for action, *which in before.get(at, []):
                    action(*which)
                ready(k, dx)

        chip = chips[0]
        for at in range(1, len(UNITS)):
            chip = jnp.where(step == at, chips[at], chip)
        keys = kv_ref[pl.ds(2 * chip, 2), 0].reshape(TILE, WIDTH)
        values = kv_ref[pl.ds(2 * chip, 2), 1].reshape(TILE, WIDTH)
        key_pos = jnp.concatenate(
            [block_row + order_ref[4 * chip + i] * BLOCK for i in range(4)], axis=0
        )
        value_side = jnp.concatenate([values, value_extra], axis=1)
        keys_turn = keys.T
        grad_keys = grad_values = None
        for half in range(2):
            hidden = (key_pos > query_pos[half]) | (key_pos < query_start[half])
            extra = jnp.where(hidden, MASKED, norm_extra).astype(BF16)
            scores = jnp.dot(
                jnp.concatenate([keys, extra], axis=1), q_turn[half], preferred_element_type=F32
            )
            weights = jnp.exp2(scores * EXP2_SCALE)
            grad_weights = jnp.dot(value_side, g_turn[half], preferred_element_type=F32)
            grad_scores = (weights * grad_weights).astype(BF16)
            to_values = jnp.dot(
                weights.astype(BF16), g_all[half, :, :WIDTH], preferred_element_type=F32
            )
            to_keys = jnp.dot(grad_scores, q_all[half, :, :WIDTH], preferred_element_type=F32)
            dq_turn[half] += jnp.dot(keys_turn, grad_scores, preferred_element_type=F32)
            grad_keys = to_keys if half == 0 else grad_keys + to_keys
            grad_values = to_values if half == 0 else grad_values + to_values
        for i in range(2):
            rows = slice(2 * i * BLOCK, 2 * (i + 1) * BLOCK)
            work[i, 0] = grad_keys[rows] * SCALE
            work[i, 1] = grad_values[rows]
        part[step] = work[me.core]
        sib_out[step] = work[1 - me.core].astype(BF16)
        copy_to(
            sib_out.at[step], sib.at[step], p_send.at[step], p_recv.at[step], sibling, head
        ).start()
        return carry

    lax.fori_loop(0, len(UNITS), unit, 0)
    give_sum(13)
    give_sum(14)
    sum_column(1)
    for half in range(2):
        dq = (dq_turn[half] * SCALE).T
        for h in range(8):
            dq_ref[half * BLOCK : (half + 1) * BLOCK, h * WIDTH : (h + 1) * WIDTH] = dq[
                h * BLOCK : (h + 1) * BLOCK
            ].astype(BF16)
    sum_column(2)
    sum_column(3)
    for i, group in enumerate(groups):
        sums = None if i else [mine_sum[j] for j in range(2)]
        for z in order[1 - i :]:
            arrived(deep.at[group, z], rz_recv.at[group, z], me.at(z))
            got = [deep[group, z, j].astype(F32) for j in range(2)]
            sums = got if sums is None else [sums[j] + got[j] for j in range(2)]
        for j in range(2):
            total[i, j] = sums[j].astype(BF16)
    outs = (dk_ref, dv_ref)
    for d in range(1, 4):
        for i, group in enumerate(groups):
            columns = head_columns(group * 4 + me.y)
            for j in range(2):
                send(
                    total.at[i, j, head_rows((me.y + d) % 4), :], outs[j].at[:, columns],
                    rh_send.at[i, j, d], rh_recv.at[i, j, d], own, me.beside_y(d),
                )
    for i, group in enumerate(groups):
        for j in range(2):
            outs[j][:, head_columns(group * 4 + me.y)] = total[i, j, head_rows(me.y), :]
    for d in range(1, 4):
        for i, group in enumerate(groups):
            for j in range(2):
                here = outs[j].at[:, head_columns(group * 4 + (me.y + 4 - d) % 4)]
                copy_to(
                    here, here, rh_send.at[i, j, d], rh_recv.at[i, j, d], own, me.beside_y(4 - d)
                ).wait_recv()
    sent += [(sib_out.shape[1:], p_send.at[step]) for step in range(len(UNITS))]
    shapes = {
        (2, 2 * BLOCK, WIDTH): kv_ref.at[0],
        (2 * BLOCK, WIDTH): kv_ref.at[0, 0],
        (2, BLOCK, WIDTH): other_ref,
        (BLOCK, WIDTH): other_ref.at[0],
        (16, WIDTH): kv_ref.at[0, 0, pl.ds(0, 16), :],
    }
    for shape, sent_sem in sent:
        block = shapes[tuple(shape)]
        copy_to(block, block, sent_sem, s_recv.at[0, 0], sibling, head).wait_send()


def backward(order, docs, queries, output, grad_out, norm_turn, key_matrix, value_matrix):
    smem = pl.BlockSpec(memory_space=pltpu.SMEM)
    vmem = pl.BlockSpec(memory_space=pltpu.VMEM)
    hbm = pl.BlockSpec(memory_space=pl.ANY)
    dma = pltpu.SemaphoreType.DMA
    chunk = (2 * BLOCK, WIDTH)
    rows = 8 * BLOCK
    out = jax.ShapeDtypeStruct(key_matrix.shape, BF16)
    return pl.pallas_call(
        backward_kernel,
        out_shape=(jax.ShapeDtypeStruct(queries.shape, BF16), out, out),
        in_specs=[smem, hbm, hbm, hbm, hbm, vmem, hbm, hbm],
        out_specs=(vmem, vmem, vmem),
        scratch_shapes=[
            pltpu.VMEM(docs.shape, jnp.int32),
            pltpu.VMEM(queries.shape, BF16),
            pltpu.VMEM(queries.shape, BF16),
            pltpu.VMEM(queries.shape, BF16),
            pltpu.VMEM(key_matrix.shape, BF16),
            pltpu.VMEM(key_matrix.shape, BF16),
            pltpu.VMEM((32, 2) + chunk, BF16),
            pltpu.VMEM((2, BLOCK, WIDTH), BF16),
            pltpu.VMEM((2, rows, 2 * WIDTH), BF16),
            pltpu.VMEM((2, rows, 2 * WIDTH), BF16),
            pltpu.VMEM((2, 2 * WIDTH, rows), BF16),
            pltpu.VMEM((2, 2 * WIDTH, rows), BF16),
            pltpu.VMEM((2, WIDTH, rows), F32),
            pltpu.VMEM((2, 2) + chunk, F32),
            pltpu.VMEM((16, 2) + chunk, F32),
            pltpu.VMEM((16, 2) + chunk, BF16),
            pltpu.VMEM((16, 2) + chunk, BF16),
            pltpu.VMEM((4, 4, 2) + chunk, BF16),
            pltpu.VMEM((2, 4, 2, BLOCK, WIDTH), BF16),
            pltpu.VMEM((4, 4, 2) + chunk, BF16),
            pltpu.VMEM((4, 2) + chunk, BF16),
            pltpu.VMEM((2, 2, BLOCK, WIDTH), BF16),
            pltpu.VMEM((2,) + chunk, F32),
            pltpu.VMEM((2, BLOCK, WIDTH), F32),
            dma((6,)),
            dma((2, 2, 4)), dma((2, 2, 4)), dma((2, 4)), dma((2, 4)), dma((4, 5)), dma((4, 5)),
            dma((5, 4)), dma((5, 4)), dma((16,)), dma((16,)), dma((4, 4)), dma((4, 4)),
            dma((2, 4)), dma((2, 4)), dma((2, 2, 4)), dma((2, 2, 4)),
        ],
        compiler_params=pltpu.CompilerParams(
            collective_id=0, has_side_effects=True, vmem_limit_bytes=56 * 2**20
        ),
        name="backward",
    )(order, docs, queries, output, grad_out, norm_turn, key_matrix, value_matrix)


def body(queries, key_matrix, value_matrix, output, grad_out, log_norm, doc_ids, block_order):
    return backward(
        block_order, doc_ids.reshape(-1, WIDTH), queries, output, grad_out, log_norm.T,
        key_matrix, value_matrix,
    )


def solution(mesh):
    placed = (
        P("blk", "head"),
        P(("blk", "head"), None),
        P(("blk", "head"), None),
        P("blk", "head"),
        P("blk", "head"),
        P("blk", "head"),
        P(),
        P(),
    )
    return jax.shard_map(
        body,
        mesh=mesh,
        in_specs=placed,
        out_specs=(P("blk", "head"), P(("blk", "head"), None), P(("blk", "head"), None)),
        check_vma=False,
    )
```

```python
import functools
import math

import jax
import jax.numpy as jnp
from jax import lax
from jax.experimental import pallas as pl
from jax.experimental.pallas import tpu as pltpu
from jax.sharding import PartitionSpec as P

WIDTH = 128
BLOCK = 64
DOCS = 6
TILE = 256
MASKED = -(2.0**17)
ROOT = math.sqrt(WIDTH)
SCALE = 1.0 / ROOT
EXP2_SCALE = SCALE * math.log2(math.e)
BF16 = jnp.bfloat16
F32 = jnp.float32


def root_parts():
    parts, rest = [], ROOT
    for _ in range(3):
        term = _to_bf16(rest)
        parts.append(term)
        rest -= term
    return parts


def _to_bf16(value):
    mantissa, exponent = math.frexp(value)
    return math.ldexp(round(mantissa * 256), exponent - 8)


ROOT_PARTS = root_parts()


class Place:
    def __init__(self):
        self.span = lax.axis_index("blk")
        self.head = lax.axis_index("head")
        self.core = self.span % 2
        self.x = (self.span // 2) % 4
        self.z = self.span // 8
        self.high, self.y = self.head // 4, self.head % 4
        self.partner = (1 - self.high) * 4 + self.y
        self.near_z = (1 + self.z % 2, (2 + 3 * self.z) % 5, 3 * (1 - self.z // 2))

    def at(self, z, dx=0, other=False):
        core = 1 - self.core if other else self.core
        return (z * 4 + (self.x + dx) % 4) * 2 + core

    def beside_y(self, d):
        return self.high * 4 + (self.y + d) % 4

    @property
    def sibling(self):
        return self.at(self.z, 0, True)


def meet(place):
    barrier = pltpu.get_barrier_semaphore()
    peers = [(place.span, place.beside_y(d)) for d in range(1, 4)]
    peers += [(place.at(z), place.head) for z in place.near_z]
    peers += [(place.at(z), place.partner) for z in (place.z,) + place.near_z]
    peers += [(place.at(place.z, dx), place.head) for dx in (1, 2, 3)]
    peers += [(place.sibling, place.head)]
    for peer in peers:
        pl.semaphore_signal(
            barrier, inc=1, device_id=peer, device_id_type=pl.DeviceIdType.MESH
        )
    pl.semaphore_wait(barrier, len(peers))


class Sent:
    def __init__(self, ref):
        self.ref = ref

    @property
    def at(self):
        return self

    def __getitem__(self, index):
        return (self.ref, index)


def copy_to(src, dst, send, recv, span, head):
    ref, index = send
    send = ref.at[index]
    return pltpu.make_async_remote_copy(
        src_ref=src, dst_ref=dst, send_sem=send, recv_sem=recv,
        device_id=(span, head), device_id_type=pl.DeviceIdType.MESH,
    )


def head_rows(head):
    return pl.ds(pl.multiple_of(head * 16, 16), 16)


def half_rows(high):
    return pl.ds(pl.multiple_of(high * BLOCK, BLOCK), BLOCK)


def head_columns(head):
    return pl.ds(pl.multiple_of(head * WIDTH, WIDTH), WIDTH)


OWN, LEFT, RIGHT, FAR = 0, 3, 1, 2
UNITS = [
    (0, OWN), (1, OWN), (2, OWN), (0, LEFT), (0, RIGHT), (0, FAR), (1, LEFT), (1, RIGHT),
    (1, FAR), (2, LEFT), (2, RIGHT), (2, FAR), (3, LEFT), (3, RIGHT), (3, FAR), (3, OWN),
]
ALL, MINE, OTHER = 0, 1, 2
ITEMS = [(0, MINE), (1, ALL), (0, OTHER), (2, ALL), (3, ALL)]
STEP_OF = {unit: step for step, unit in enumerate(UNITS)}


def backward_kernel(
    order_ref, docs_hbm, q_hbm, o_hbm, g_hbm, norm_ref, k_hbm, v_hbm,
    dq_ref, dk_ref, dv_ref,
    docs_ref, q_ref, o_ref, g_ref, k_ref, v_ref,
    kv_ref, other_ref, q_all, g_all, q_turn, g_turn, dq_turn, work,
    part, sib_out, sib, near, deep, near_out, deep_out, total, deep_sum, mine_sum,
    load_sem,
    head_send, head_recv, z_send, z_recv, x_send, x_recv, s_send, s_recv,
    p_send, p_recv, rx_send, rx_recv, rz_send, rz_recv, rh_send, rh_recv,
):
    head_send, z_send, x_send, s_send, p_send, rx_send, rz_send, rh_send = map(
        Sent, (head_send, z_send, x_send, s_send, p_send, rx_send, rz_send, rh_send)
    )
    me = Place()
    own, head = me.span, me.head
    order = (me.z,) + me.near_z
    sibling = me.sibling

    loads = [
        pltpu.make_async_copy(src, dst, load_sem.at[i])
        for i, (src, dst) in enumerate(
            (
                (k_hbm, k_ref), (v_hbm, v_ref), (q_hbm, q_ref), (g_hbm, g_ref),
                (o_hbm, o_ref), (docs_hbm, docs_ref),
            )
        )
    ]
    for load in loads:
        load.start()
    meet(me)
    loads[0].wait()
    loads[1].wait()

    sent = []

    def send(src, dst, sent_sem, recv_sem, span, to_head):
        copy_to(src, dst, sent_sem, recv_sem, span, to_head).start()
        sent.append((src.shape, sent_sem))

    def arrived(block, recv, span):
        copy_to(block, block, s_send.at[0, 0], recv, span, head).wait_recv()

    homes = (kv_ref.at[own, :, half_rows(me.high), :], other_ref)
    groups = (me.high, 1 - me.high)
    for d in range(1, 4):
        to = me.beside_y(d)
        for i, (home, group) in enumerate(zip(homes, groups)):
            columns = head_columns(group * 4 + (me.y + d) % 4)
            for j, ref in enumerate((k_ref, v_ref)):
                send(
                    ref.at[:, columns], home.at[j, head_rows(me.y), :],
                    head_send.at[i, j, d], head_recv.at[i, j, d], own, to,
                )
    for j, ref in enumerate((k_ref, v_ref)):
        kv_ref[own, j, head_rows(head), :] = ref[:, head_columns(head)]
        other_ref[j, head_rows(me.y), :] = ref[:, head_columns(me.partner)]

    for load in loads[2:]:
        load.wait()
    docs = docs_ref[...]
    starts = [jnp.sum((docs < d).astype(jnp.int32)) for d in range(1, DOCS)]
    lane = lax.broadcasted_iota(jnp.int32, (BLOCK, WIDTH), 1)
    row = lax.broadcasted_iota(jnp.int32, (BLOCK, WIDTH), 0)
    one_hot = (lane == row).astype(F32)
    norm_lane = (lane >= BLOCK) & (lane < BLOCK + 3)
    lanes = lax.broadcasted_iota(jnp.int32, (1, WIDTH), 1)
    norms = norm_ref[...].astype(F32).T
    query_pos, query_start = [], []

    def prepare(half):
        here = slice(half * BLOCK, (half + 1) * BLOCK)
        for h in range(8):
            cols = slice(h * WIDTH, (h + 1) * WIDTH)
            there = slice(h * BLOCK, (h + 1) * BLOCK)
            g = g_ref[here, cols]
            q_all[half, there, :WIDTH] = q_ref[here, cols]
            g_all[half, there, :WIDTH] = g
            norm = norms[here, h : h + 1]
            q_all[half, there, WIDTH:] = jnp.where(norm_lane, norm, one_hot).astype(BF16)
            delta = jnp.sum(g.astype(F32) * o_ref[here, cols].astype(F32), axis=1, keepdims=True)
            high = delta.astype(BF16).astype(F32)
            mid = (delta - high).astype(BF16).astype(F32)
            low = delta - high - mid
            extra = jnp.where(
                lane == 0, high, jnp.where(lane == 1, mid, jnp.where(lane == 2, low, 0.0))
            )
            g_all[half, there, WIDTH:] = extra.astype(BF16)
        q_turn[half] = q_all[half].T
        g_turn[half] = g_all[half].T
        dq_turn[half] = jnp.zeros((WIDTH, 8 * BLOCK), F32)
        pos = lanes + order_ref[2 * own + half] * BLOCK
        start = jnp.zeros_like(pos)
        for s in starts:
            start = jnp.maximum(start, jnp.where(s <= pos, s, 0))
        query_pos.append(jnp.where(lanes < BLOCK, pos, 1 << 20))
        query_start.append(jnp.where(lanes < BLOCK, start, 0))

    prepare(0)
    tile_lane = lax.broadcasted_iota(jnp.int32, (TILE, WIDTH), 1)
    value_extra = jnp.where(tile_lane < 3, -1.0, 0.0).astype(BF16)
    norm_extra = jnp.zeros((1, WIDTH), F32)
    for i, term in enumerate(ROOT_PARTS):
        norm_extra = jnp.where(lanes == BLOCK + i, -term, norm_extra)

    for d in range(1, 4):
        source = me.beside_y(4 - d)
        for i, home in enumerate(homes):
            for j in range(2):
                here = home.at[j, head_rows((me.y + 4 - d) % 4), :]
                copy_to(
                    here, here, head_send.at[i, j, d], head_recv.at[i, j, d], own, source
                ).wait_recv()

    def give_deep(k):
        if k > 0:
            send(
                homes[0], homes[0], z_send.at[0, k], z_recv.at[me.high, me.z],
                me.at(order[k]), head,
            )
        send(
            other_ref, homes[0], z_send.at[1, k], z_recv.at[me.high, me.z],
            me.at(order[k]), me.partner,
        )

    def item(i, dx, other=False):
        k, which = ITEMS[i]
        block = kv_ref.at[me.at(order[k], dx, other)]
        if which == ALL:
            return block
        return block.at[:, half_rows(me.high if which == MINE else 1 - me.high), :]

    def over(block, i, which):
        send(block, block, s_send.at[i, which], s_recv.at[i, which], sibling, head)

    def give_column(i):
        k, which = ITEMS[i]
        span = me.at(order[k])
        for high in (me.high, 1 - me.high):
            if which == ALL or (which == OTHER and high is not me.high):
                half = kv_ref.at[span, :, half_rows(high), :]
                arrived(half, z_recv.at[high, order[k]], span)
        block = item(i, OWN)
        for dx in (FAR, RIGHT, LEFT):
            send(block, block, x_send.at[dx, i], x_recv.at[dx, i], me.at(me.z, dx), head)
        over(block, i, OWN)

    def give_on(i, *steps):
        for dx in steps:
            block = item(i, dx)
            arrived(block, x_recv.at[4 - dx, i], me.at(me.z, dx))
            over(block, i, dx)

    def ready(k, dx):
        for i, (at, _) in enumerate(ITEMS):
            if at != k:
                continue
            arrived(item(i, dx, True), s_recv.at[i, dx], sibling)

    def pair(k, dx, j):
        step = STEP_OF[k, dx]
        return part[step, j] + sib[step, j].astype(F32)

    def met(k, dx):
        step = STEP_OF[k, dx]
        arrived(sib.at[step], p_recv.at[step], sibling)

    def give_sum(step):
        k, dx = UNITS[step]
        met(k, dx)
        for j in range(2):
            near_out[dx, k, j] = pair(k, dx, j).astype(BF16)
        send(
            near_out.at[dx, k], near.at[dx, k], rx_send.at[dx, k], rx_recv.at[dx, k],
            me.at(me.z, dx), head,
        )

    def sum_column(k):
        met(k, OWN)
        sums = [pair(k, OWN, j) for j in range(2)]
        for dx in (LEFT, RIGHT, FAR):
            arrived(near.at[dx, k], rx_recv.at[dx, k], me.at(me.z, 4 - dx))
            sums = [sums[j] + near[dx, k, j].astype(F32) for j in range(2)]
        for j in range(2):
            deep_out[k, j] = sums[j].astype(BF16)
        if k == 0:
            for j in range(2):
                deep_sum[j] = sums[j]
                mine_sum[j] = deep_sum[j, half_rows(me.high), :]
        for i, to in enumerate((head, me.partner)):
            if k > 0 or i > 0:
                send(
                    deep_out.at[k, :, half_rows(me.high if i == 0 else 1 - me.high), :],
                    deep.at[me.high, me.z], rz_send.at[i, k], rz_recv.at[me.high, me.z],
                    me.at(order[k]), to,
                )

    before = {
        0: [(give_column, 1), (give_column, 2)],
        1: [(give_on, 0, LEFT, RIGHT), (give_column, 3)],
        2: [(give_on, 0, FAR), (give_column, 4)],
        3: [(give_on, 2, LEFT, RIGHT), (give_on, 1, LEFT, RIGHT)],
        4: [(give_on, 2, FAR), (give_on, 1, FAR)],
        6: [(give_sum, 3)],
        7: [(give_sum, 4), (give_on, 3, LEFT, RIGHT)],
        8: [(give_sum, 5), (give_on, 3, FAR)],
        9: [(give_sum, 6)],
        10: [(give_sum, 7), (give_on, 4, LEFT, RIGHT)],
        11: [(give_sum, 8), (give_on, 4, FAR)],
        12: [(give_sum, 9)],
        13: [(give_sum, 10)],
        14: [(give_sum, 11), (sum_column, 0)],
        15: [(give_sum, 12)],
    }
    chips = [order[k] * 4 + (me.x + dx) % 4 for k, dx in UNITS]
    give_deep(1)
    give_deep(0)
    give_column(0)
    prepare(1)
    give_deep(2)
    give_deep(3)
    block_row = lax.broadcasted_iota(jnp.int32, (BLOCK, WIDTH), 0)

    def unit(step, carry):
        for at, (k, dx) in enumerate(UNITS):

            @pl.when(step == at)
            def _():
                for action, *which in before.get(at, []):
                    action(*which)
                ready(k, dx)

        chip = chips[0]
        for at in range(1, len(UNITS)):
            chip = jnp.where(step == at, chips[at], chip)
        keys = kv_ref[pl.ds(2 * chip, 2), 0].reshape(TILE, WIDTH)
        values = kv_ref[pl.ds(2 * chip, 2), 1].reshape(TILE, WIDTH)
        key_pos = jnp.concatenate(
            [block_row + order_ref[4 * chip + i] * BLOCK for i in range(4)], axis=0
        )
        value_side = jnp.concatenate([values, value_extra], axis=1)
        keys_turn = keys.T
        scores, grad_weights = [], []
        for half in range(2):
            hidden = (key_pos > query_pos[half]) | (key_pos < query_start[half])
            extra = jnp.where(hidden, MASKED, norm_extra).astype(BF16)
            scores.append(
                jnp.dot(
                    jnp.concatenate([keys, extra], axis=1), q_turn[half],
                    preferred_element_type=F32,
                )
            )
            grad_weights.append(jnp.dot(value_side, g_turn[half], preferred_element_type=F32))
        weights = [jnp.exp2(score * EXP2_SCALE) for score in scores]
        grad_scores = [(weights[half] * grad_weights[half]).astype(BF16) for half in range(2)]
        grad_values = sum(
            jnp.dot(weights[half].astype(BF16), g_all[half, :, :WIDTH], preferred_element_type=F32)
            for half in range(2)
        )
        grad_keys = sum(
            jnp.dot(grad_scores[half], q_all[half, :, :WIDTH], preferred_element_type=F32)
            for half in range(2)
        )
        for half in range(2):
            dq_turn[half] += jnp.dot(keys_turn, grad_scores[half], preferred_element_type=F32)
        for i in range(2):
            rows = slice(2 * i * BLOCK, 2 * (i + 1) * BLOCK)
            work[i, 0] = grad_keys[rows] * SCALE
            work[i, 1] = grad_values[rows]
        part[step] = work[me.core]
        sib_out[step] = work[1 - me.core].astype(BF16)
        copy_to(
            sib_out.at[step], sib.at[step], p_send.at[step], p_recv.at[step], sibling, head
        ).start()
        return carry

    lax.fori_loop(0, len(UNITS), unit, 0)
    give_sum(13)
    give_sum(14)
    sum_column(1)
    for half in range(2):
        dq = (dq_turn[half] * SCALE).T
        for h in range(8):
            dq_ref[half * BLOCK : (half + 1) * BLOCK, h * WIDTH : (h + 1) * WIDTH] = dq[
                h * BLOCK : (h + 1) * BLOCK
            ].astype(BF16)
    sum_column(2)
    sum_column(3)
    for i, group in enumerate(groups):
        sums = None if i else [mine_sum[j] for j in range(2)]
        for z in order[1 - i :]:
            arrived(deep.at[group, z], rz_recv.at[group, z], me.at(z))
            got = [deep[group, z, j].astype(F32) for j in range(2)]
            sums = got if sums is None else [sums[j] + got[j] for j in range(2)]
        for j in range(2):
            total[i, j] = sums[j].astype(BF16)
    outs = (dk_ref, dv_ref)
    for d in range(1, 4):
        for i, group in enumerate(groups):
            columns = head_columns(group * 4 + me.y)
            for j in range(2):
                send(
                    total.at[i, j, head_rows((me.y + d) % 4), :], outs[j].at[:, columns],
                    rh_send.at[i, j, d], rh_recv.at[i, j, d], own, me.beside_y(d),
                )
    for i, group in enumerate(groups):
        for j in range(2):
            outs[j][:, head_columns(group * 4 + me.y)] = total[i, j, head_rows(me.y), :]
    for d in range(1, 4):
        for i, group in enumerate(groups):
            for j in range(2):
                here = outs[j].at[:, head_columns(group * 4 + (me.y + 4 - d) % 4)]
                copy_to(
                    here, here, rh_send.at[i, j, d], rh_recv.at[i, j, d], own, me.beside_y(4 - d)
                ).wait_recv()
    sent += [(sib_out.shape[1:], p_send.at[step]) for step in range(len(UNITS))]
    shapes = {
        (2, 2 * BLOCK, WIDTH): kv_ref.at[0],
        (2 * BLOCK, WIDTH): kv_ref.at[0, 0],
        (2, BLOCK, WIDTH): other_ref,
        (BLOCK, WIDTH): other_ref.at[0],
        (16, WIDTH): kv_ref.at[0, 0, pl.ds(0, 16), :],
    }
    for shape, sent_sem in sent:
        block = shapes[tuple(shape)]
        copy_to(block, block, sent_sem, s_recv.at[0, 0], sibling, head).wait_send()


def backward(order, docs, queries, output, grad_out, norm_turn, key_matrix, value_matrix):
    smem = pl.BlockSpec(memory_space=pltpu.SMEM)
    vmem = pl.BlockSpec(memory_space=pltpu.VMEM)
    hbm = pl.BlockSpec(memory_space=pl.ANY)
    dma = pltpu.SemaphoreType.DMA
    chunk = (2 * BLOCK, WIDTH)
    rows = 8 * BLOCK
    out = jax.ShapeDtypeStruct(key_matrix.shape, BF16)
    return pl.pallas_call(
        backward_kernel,
        out_shape=(jax.ShapeDtypeStruct(queries.shape, BF16), out, out),
        in_specs=[smem, hbm, hbm, hbm, hbm, vmem, hbm, hbm],
        out_specs=(vmem, vmem, vmem),
        scratch_shapes=[
            pltpu.VMEM(docs.shape, jnp.int32),
            pltpu.VMEM(queries.shape, BF16),
            pltpu.VMEM(queries.shape, BF16),
            pltpu.VMEM(queries.shape, BF16),
            pltpu.VMEM(key_matrix.shape, BF16),
            pltpu.VMEM(key_matrix.shape, BF16),
            pltpu.VMEM((32, 2) + chunk, BF16),
            pltpu.VMEM((2, BLOCK, WIDTH), BF16),
            pltpu.VMEM((2, rows, 2 * WIDTH), BF16),
            pltpu.VMEM((2, rows, 2 * WIDTH), BF16),
            pltpu.VMEM((2, 2 * WIDTH, rows), BF16),
            pltpu.VMEM((2, 2 * WIDTH, rows), BF16),
            pltpu.VMEM((2, WIDTH, rows), F32),
            pltpu.VMEM((2, 2) + chunk, F32),
            pltpu.VMEM((16, 2) + chunk, F32),
            pltpu.VMEM((16, 2) + chunk, BF16),
            pltpu.VMEM((16, 2) + chunk, BF16),
            pltpu.VMEM((4, 4, 2) + chunk, BF16),
            pltpu.VMEM((2, 4, 2, BLOCK, WIDTH), BF16),
            pltpu.VMEM((4, 4, 2) + chunk, BF16),
            pltpu.VMEM((4, 2) + chunk, BF16),
            pltpu.VMEM((2, 2, BLOCK, WIDTH), BF16),
            pltpu.VMEM((2,) + chunk, F32),
            pltpu.VMEM((2, BLOCK, WIDTH), F32),
            dma((6,)),
            dma((2, 2, 4)), dma((2, 2, 4)), dma((2, 4)), dma((2, 4)), dma((4, 5)), dma((4, 5)),
            dma((5, 4)), dma((5, 4)), dma((16,)), dma((16,)), dma((4, 4)), dma((4, 4)),
            dma((2, 4)), dma((2, 4)), dma((2, 2, 4)), dma((2, 2, 4)),
        ],
        compiler_params=pltpu.CompilerParams(
            collective_id=0, has_side_effects=True, vmem_limit_bytes=56 * 2**20
        ),
        name="backward",
    )(order, docs, queries, output, grad_out, norm_turn, key_matrix, value_matrix)


def hand_out_kernel(dq_ref, dk_ref, dv_ref, dq_out, dk_out, dv_out, sem):
    pairs = ((dq_ref, dq_out), (dk_ref, dk_out), (dv_ref, dv_out))
    copies = [pltpu.make_async_copy(src, dst, sem.at[i]) for i, (src, dst) in enumerate(pairs)]
    for copy in copies:
        copy.start()
    for copy in copies:
        copy.wait()


def hand_out(*grads):
    hbm = pl.BlockSpec(memory_space=pl.ANY)
    return pl.pallas_call(
        hand_out_kernel,
        out_shape=tuple(jax.ShapeDtypeStruct(grad.shape, grad.dtype) for grad in grads),
        in_specs=[pl.BlockSpec(memory_space=pltpu.VMEM)] * 3,
        out_specs=(hbm,) * 3,
        scratch_shapes=[pltpu.SemaphoreType.DMA((3,))],
        name="hand_out",
    )(*grads)


def body(queries, key_matrix, value_matrix, output, grad_out, log_norm, doc_ids, block_order):
    grads = backward(
        block_order, doc_ids.reshape(-1, WIDTH), queries, output, grad_out, log_norm.T,
        key_matrix, value_matrix,
    )
    return hand_out(*grads)


def solution(mesh):
    placed = (
        P("blk", "head"),
        P(("blk", "head"), None),
        P(("blk", "head"), None),
        P("blk", "head"),
        P("blk", "head"),
        P("blk", "head"),
        P(),
        P(),
    )
    return jax.shard_map(
        body,
        mesh=mesh,
        in_specs=placed,
        out_specs=(P("blk", "head"), P(("blk", "head"), None), P(("blk", "head"), None)),
        check_vma=False,
    )
```

```python
import functools
import math

import jax
import jax.numpy as jnp
from jax import lax
from jax.experimental import pallas as pl
from jax.experimental.pallas import tpu as pltpu
from jax.sharding import PartitionSpec as P

WIDTH = 128
BLOCK = 64
DOCS = 6
TILE = 256
MASKED = -(2.0**17)
ROOT = math.sqrt(WIDTH)
SCALE = 1.0 / ROOT
EXP2_SCALE = SCALE * math.log2(math.e)
BF16 = jnp.bfloat16
F32 = jnp.float32


def root_parts():
    parts, rest = [], ROOT
    for _ in range(3):
        term = _to_bf16(rest)
        parts.append(term)
        rest -= term
    return parts


def _to_bf16(value):
    mantissa, exponent = math.frexp(value)
    return math.ldexp(round(mantissa * 256), exponent - 8)


ROOT_PARTS = root_parts()


class Place:
    def __init__(self):
        self.span = lax.axis_index("blk")
        self.head = lax.axis_index("head")
        self.core = self.span % 2
        self.x = (self.span // 2) % 4
        self.z = self.span // 8
        self.high, self.y = self.head // 4, self.head % 4
        self.partner = (1 - self.high) * 4 + self.y
        self.near_z = (1 + self.z % 2, (2 + 3 * self.z) % 5, 3 * (1 - self.z // 2))

    def at(self, z, dx=0, other=False):
        core = 1 - self.core if other else self.core
        return (z * 4 + (self.x + dx) % 4) * 2 + core

    def beside_y(self, d):
        return self.high * 4 + (self.y + d) % 4

    @property
    def sibling(self):
        return self.at(self.z, 0, True)


def meet(place):
    barrier = pltpu.get_barrier_semaphore()
    peers = [(place.span, place.beside_y(d)) for d in range(1, 4)]
    peers += [(place.at(z), place.head) for z in place.near_z]
    peers += [(place.at(z), place.partner) for z in (place.z,) + place.near_z]
    peers += [(place.at(place.z, dx), place.head) for dx in (1, 2, 3)]
    peers += [(place.sibling, place.head)]
    for peer in peers:
        pl.semaphore_signal(
            barrier, inc=1, device_id=peer, device_id_type=pl.DeviceIdType.MESH
        )
    return lambda: pl.semaphore_wait(barrier, len(peers))


class Sent:
    def __init__(self, ref):
        self.ref = ref

    @property
    def at(self):
        return self

    def __getitem__(self, index):
        return (self.ref, index)


def copy_to(src, dst, send, recv, span, head):
    ref, index = send
    send = ref.at[index]
    return pltpu.make_async_remote_copy(
        src_ref=src, dst_ref=dst, send_sem=send, recv_sem=recv,
        device_id=(span, head), device_id_type=pl.DeviceIdType.MESH,
    )


def head_rows(head):
    return pl.ds(pl.multiple_of(head * 16, 16), 16)


def half_rows(high):
    return pl.ds(pl.multiple_of(high * BLOCK, BLOCK), BLOCK)


def head_columns(head):
    return pl.ds(pl.multiple_of(head * WIDTH, WIDTH), WIDTH)


OWN, LEFT, RIGHT, FAR = 0, 3, 1, 2
UNITS = [
    (0, OWN), (1, OWN), (2, OWN), (0, LEFT), (0, RIGHT), (0, FAR), (1, LEFT), (1, RIGHT),
    (1, FAR), (2, LEFT), (2, RIGHT), (2, FAR), (3, LEFT), (3, RIGHT), (3, FAR), (3, OWN),
]
ALL, MINE, OTHER = 0, 1, 2
ITEMS = [(0, MINE), (1, ALL), (0, OTHER), (2, ALL), (3, ALL)]
STEP_OF = {unit: step for step, unit in enumerate(UNITS)}


def backward_kernel(
    order_ref, docs_hbm, q_hbm, o_hbm, g_hbm, norm_ref, k_hbm, v_hbm,
    dq_ref, dk_ref, dv_ref,
    docs_ref, q_ref, o_ref, g_ref, k_ref, v_ref,
    kv_ref, other_ref, q_all, g_all, q_turn, g_turn, dq_turn, work,
    part, sib_out, sib, near, deep, near_out, deep_out, total, deep_sum, mine_sum,
    load_sem,
    head_send, head_recv, z_send, z_recv, x_send, x_recv, s_send, s_recv,
    p_send, p_recv, rx_send, rx_recv, rz_send, rz_recv, rh_send, rh_recv,
):
    head_send, z_send, x_send, s_send, p_send, rx_send, rz_send, rh_send = map(
        Sent, (head_send, z_send, x_send, s_send, p_send, rx_send, rz_send, rh_send)
    )
    me = Place()
    own, head = me.span, me.head
    order = (me.z,) + me.near_z
    sibling = me.sibling

    all_here = meet(me)
    loads = [
        pltpu.make_async_copy(src, dst, load_sem.at[i])
        for i, (src, dst) in enumerate(
            (
                (k_hbm, k_ref), (v_hbm, v_ref), (q_hbm, q_ref), (g_hbm, g_ref),
                (o_hbm, o_ref), (docs_hbm, docs_ref),
            )
        )
    ]
    for load in loads:
        load.start()
    all_here()
    loads[0].wait()
    loads[1].wait()

    sent = []

    def send(src, dst, sent_sem, recv_sem, span, to_head):
        copy_to(src, dst, sent_sem, recv_sem, span, to_head).start()
        sent.append((src.shape, sent_sem))

    def arrived(block, recv, span):
        copy_to(block, block, s_send.at[0, 0], recv, span, head).wait_recv()

    homes = (kv_ref.at[own, :, half_rows(me.high), :], other_ref)
    groups = (me.high, 1 - me.high)
    for d in range(1, 4):
        to = me.beside_y(d)
        for i, (home, group) in enumerate(zip(homes, groups)):
            columns = head_columns(group * 4 + (me.y + d) % 4)
            for j, ref in enumerate((k_ref, v_ref)):
                send(
                    ref.at[:, columns], home.at[j, head_rows(me.y), :],
                    head_send.at[i, j, d], head_recv.at[i, j, d], own, to,
                )
    for j, ref in enumerate((k_ref, v_ref)):
        kv_ref[own, j, head_rows(head), :] = ref[:, head_columns(head)]
        other_ref[j, head_rows(me.y), :] = ref[:, head_columns(me.partner)]

    for d in range(1, 4):
        source = me.beside_y(4 - d)
        for i, home in enumerate(homes):
            for j in range(2):
                here = home.at[j, head_rows((me.y + 4 - d) % 4), :]
                copy_to(
                    here, here, head_send.at[i, j, d], head_recv.at[i, j, d], own, source
                ).wait_recv()

    def give_deep(k):
        if k > 0:
            send(
                homes[0], homes[0], z_send.at[0, k], z_recv.at[me.high, me.z],
                me.at(order[k]), head,
            )
        send(
            other_ref, homes[0], z_send.at[1, k], z_recv.at[me.high, me.z],
            me.at(order[k]), me.partner,
        )

    def item(i, dx, other=False):
        k, which = ITEMS[i]
        block = kv_ref.at[me.at(order[k], dx, other)]
        if which == ALL:
            return block
        return block.at[:, half_rows(me.high if which == MINE else 1 - me.high), :]

    def over(block, i, which):
        send(block, block, s_send.at[i, which], s_recv.at[i, which], sibling, head)

    def give_column(i):
        k, which = ITEMS[i]
        span = me.at(order[k])
        for high in (me.high, 1 - me.high):
            if which == ALL or (which == OTHER and high is not me.high):
                half = kv_ref.at[span, :, half_rows(high), :]
                arrived(half, z_recv.at[high, order[k]], span)
        block = item(i, OWN)
        for dx in (FAR, RIGHT, LEFT):
            send(block, block, x_send.at[dx, i], x_recv.at[dx, i], me.at(me.z, dx), head)
        over(block, i, OWN)

    def give_on(i, *steps):
        for dx in steps:
            block = item(i, dx)
            arrived(block, x_recv.at[4 - dx, i], me.at(me.z, dx))
            over(block, i, dx)

    def ready(k, dx):
        for i, (at, _) in enumerate(ITEMS):
            if at != k:
                continue
            arrived(item(i, dx, True), s_recv.at[i, dx], sibling)

    def pair(k, dx, j):
        step = STEP_OF[k, dx]
        return part[step, j] + sib[step, j].astype(F32)

    def met(k, dx):
        step = STEP_OF[k, dx]
        arrived(sib.at[step], p_recv.at[step], sibling)

    def give_sum(step):
        k, dx = UNITS[step]
        met(k, dx)
        for j in range(2):
            near_out[dx, k, j] = pair(k, dx, j).astype(BF16)
        send(
            near_out.at[dx, k], near.at[dx, k], rx_send.at[dx, k], rx_recv.at[dx, k],
            me.at(me.z, dx), head,
        )

    def sum_column(k):
        met(k, OWN)
        sums = [pair(k, OWN, j) for j in range(2)]
        for dx in (LEFT, RIGHT, FAR):
            arrived(near.at[dx, k], rx_recv.at[dx, k], me.at(me.z, 4 - dx))
            sums = [sums[j] + near[dx, k, j].astype(F32) for j in range(2)]
        for j in range(2):
            deep_out[k, j] = sums[j].astype(BF16)
        if k == 0:
            for j in range(2):
                deep_sum[j] = sums[j]
                mine_sum[j] = deep_sum[j, half_rows(me.high), :]
        for i, to in enumerate((head, me.partner)):
            if k > 0 or i > 0:
                send(
                    deep_out.at[k, :, half_rows(me.high if i == 0 else 1 - me.high), :],
                    deep.at[me.high, me.z], rz_send.at[i, k], rz_recv.at[me.high, me.z],
                    me.at(order[k]), to,
                )

    before = {
        0: [(give_column, 1), (give_column, 2)],
        1: [(give_on, 0, LEFT, RIGHT), (give_column, 3)],
        2: [(give_on, 0, FAR), (give_column, 4)],
        3: [(give_on, 2, LEFT, RIGHT), (give_on, 1, LEFT, RIGHT)],
        4: [(give_on, 2, FAR), (give_on, 1, FAR)],
        6: [(give_sum, 3)],
        7: [(give_sum, 4), (give_on, 3, LEFT, RIGHT)],
        8: [(give_sum, 5), (give_on, 3, FAR)],
        9: [(give_sum, 6)],
        10: [(give_sum, 7), (give_on, 4, LEFT, RIGHT)],
        11: [(give_sum, 8), (give_on, 4, FAR)],
        12: [(give_sum, 9)],
        13: [(give_sum, 10)],
        14: [(give_sum, 11), (sum_column, 0)],
        15: [(give_sum, 12)],
    }
    chips = [order[k] * 4 + (me.x + dx) % 4 for k, dx in UNITS]
    give_deep(1)
    give_deep(0)
    give_column(0)
    for load in loads[2:]:
        load.wait()
    docs = docs_ref[...]
    starts = [jnp.sum((docs < d).astype(jnp.int32)) for d in range(1, DOCS)]
    lane = lax.broadcasted_iota(jnp.int32, (BLOCK, WIDTH), 1)
    row = lax.broadcasted_iota(jnp.int32, (BLOCK, WIDTH), 0)
    one_hot = (lane == row).astype(F32)
    norm_lane = (lane >= BLOCK) & (lane < BLOCK + 3)
    lanes = lax.broadcasted_iota(jnp.int32, (1, WIDTH), 1)
    norms = norm_ref[...].astype(F32).T
    query_pos, query_start = [], []

    def prepare(half):
        here = slice(half * BLOCK, (half + 1) * BLOCK)
        for h in range(8):
            cols = slice(h * WIDTH, (h + 1) * WIDTH)
            there = slice(h * BLOCK, (h + 1) * BLOCK)
            g = g_ref[here, cols]
            q_all[half, there, :WIDTH] = q_ref[here, cols]
            g_all[half, there, :WIDTH] = g
            norm = norms[here, h : h + 1]
            q_all[half, there, WIDTH:] = jnp.where(norm_lane, norm, one_hot).astype(BF16)
            delta = jnp.sum(g.astype(F32) * o_ref[here, cols].astype(F32), axis=1, keepdims=True)
            high = delta.astype(BF16).astype(F32)
            mid = (delta - high).astype(BF16).astype(F32)
            low = delta - high - mid
            extra = jnp.where(
                lane == 0, high, jnp.where(lane == 1, mid, jnp.where(lane == 2, low, 0.0))
            )
            g_all[half, there, WIDTH:] = extra.astype(BF16)
        q_turn[half] = q_all[half].T
        g_turn[half] = g_all[half].T
        dq_turn[half] = jnp.zeros((WIDTH, 8 * BLOCK), F32)
        pos = lanes + order_ref[2 * own + half] * BLOCK
        start = jnp.zeros_like(pos)
        for s in starts:
            start = jnp.maximum(start, jnp.where(s <= pos, s, 0))
        query_pos.append(jnp.where(lanes < BLOCK, pos, 1 << 20))
        query_start.append(jnp.where(lanes < BLOCK, start, 0))

    prepare(0)
    give_deep(2)
    give_deep(3)
    prepare(1)
    tile_lane = lax.broadcasted_iota(jnp.int32, (TILE, WIDTH), 1)
    value_extra = jnp.where(tile_lane < 3, -1.0, 0.0).astype(BF16)
    norm_extra = jnp.zeros((1, WIDTH), F32)
    for i, term in enumerate(ROOT_PARTS):
        norm_extra = jnp.where(lanes == BLOCK + i, -term, norm_extra)

    block_row = lax.broadcasted_iota(jnp.int32, (BLOCK, WIDTH), 0)

    def unit(step, carry):
        for at, (k, dx) in enumerate(UNITS):

            @pl.when(step == at)
            def _():
                for action, *which in before.get(at, []):
                    action(*which)
                ready(k, dx)

        chip = chips[0]
        for at in range(1, len(UNITS)):
            chip = jnp.where(step == at, chips[at], chip)
        keys = kv_ref[pl.ds(2 * chip, 2), 0].reshape(TILE, WIDTH)
        values = kv_ref[pl.ds(2 * chip, 2), 1].reshape(TILE, WIDTH)
        key_pos = jnp.concatenate(
            [block_row + order_ref[4 * chip + i] * BLOCK for i in range(4)], axis=0
        )
        value_side = jnp.concatenate([values, value_extra], axis=1)
        keys_turn = keys.T
        scores = []
        for half in range(2):
            hidden = (key_pos > query_pos[half]) | (key_pos < query_start[half])
            extra = jnp.where(hidden, MASKED, norm_extra).astype(BF16)
            scores.append(
                jnp.dot(
                    jnp.concatenate([keys, extra], axis=1), q_turn[half],
                    preferred_element_type=F32,
                )
            )
        weights = [jnp.exp2(score * EXP2_SCALE) for score in scores]
        grad_weights = [
            jnp.dot(value_side, g_turn[half], preferred_element_type=F32) for half in range(2)
        ]
        grad_values = sum(
            jnp.dot(weights[half].astype(BF16), g_all[half, :, :WIDTH], preferred_element_type=F32)
            for half in range(2)
        )
        grad_scores = [(weights[half] * grad_weights[half]).astype(BF16) for half in range(2)]
        grad_keys = sum(
            jnp.dot(grad_scores[half], q_all[half, :, :WIDTH], preferred_element_type=F32)
            for half in range(2)
        )
        for half in range(2):
            dq_turn[half] += jnp.dot(keys_turn, grad_scores[half], preferred_element_type=F32)
        for i in range(2):
            rows = slice(2 * i * BLOCK, 2 * (i + 1) * BLOCK)
            work[i, 0] = grad_keys[rows] * SCALE
            work[i, 1] = grad_values[rows]
        part[step] = work[me.core]
        sib_out[step] = work[1 - me.core].astype(BF16)
        copy_to(
            sib_out.at[step], sib.at[step], p_send.at[step], p_recv.at[step], sibling, head
        ).start()
        return carry

    lax.fori_loop(0, len(UNITS), unit, 0)
    give_sum(13)
    give_sum(14)
    sum_column(1)
    for half in range(2):
        dq = (dq_turn[half] * SCALE).T
        for h in range(8):
            dq_ref[half * BLOCK : (half + 1) * BLOCK, h * WIDTH : (h + 1) * WIDTH] = dq[
                h * BLOCK : (h + 1) * BLOCK
            ].astype(BF16)
    sum_column(2)
    sum_column(3)
    for i, group in enumerate(groups):
        sums = None if i else [mine_sum[j] for j in range(2)]
        for z in order[1 - i :]:
            arrived(deep.at[group, z], rz_recv.at[group, z], me.at(z))
            got = [deep[group, z, j].astype(F32) for j in range(2)]
            sums = got if sums is None else [sums[j] + got[j] for j in range(2)]
        for j in range(2):
            total[i, j] = sums[j].astype(BF16)
    outs = (dk_ref, dv_ref)
    for d in range(1, 4):
        for i, group in enumerate(groups):
            columns = head_columns(group * 4 + me.y)
            for j in range(2):
                send(
                    total.at[i, j, head_rows((me.y + d) % 4), :], outs[j].at[:, columns],
                    rh_send.at[i, j, d], rh_recv.at[i, j, d], own, me.beside_y(d),
                )
    for i, group in enumerate(groups):
        for j in range(2):
            outs[j][:, head_columns(group * 4 + me.y)] = total[i, j, head_rows(me.y), :]
    for d in range(1, 4):
        for i, group in enumerate(groups):
            for j in range(2):
                here = outs[j].at[:, head_columns(group * 4 + (me.y + 4 - d) % 4)]
                copy_to(
                    here, here, rh_send.at[i, j, d], rh_recv.at[i, j, d], own, me.beside_y(4 - d)
                ).wait_recv()
    sent += [(sib_out.shape[1:], p_send.at[step]) for step in range(len(UNITS))]
    shapes = {
        (2, 2 * BLOCK, WIDTH): kv_ref.at[0],
        (2 * BLOCK, WIDTH): kv_ref.at[0, 0],
        (2, BLOCK, WIDTH): other_ref,
        (BLOCK, WIDTH): other_ref.at[0],
        (16, WIDTH): kv_ref.at[0, 0, pl.ds(0, 16), :],
    }
    for shape, sent_sem in sent:
        block = shapes[tuple(shape)]
        copy_to(block, block, sent_sem, s_recv.at[0, 0], sibling, head).wait_send()


def backward(order, docs, queries, output, grad_out, norm_turn, key_matrix, value_matrix):
    smem = pl.BlockSpec(memory_space=pltpu.SMEM)
    vmem = pl.BlockSpec(memory_space=pltpu.VMEM)
    hbm = pl.BlockSpec(memory_space=pl.ANY)
    dma = pltpu.SemaphoreType.DMA
    chunk = (2 * BLOCK, WIDTH)
    rows = 8 * BLOCK
    out = jax.ShapeDtypeStruct(key_matrix.shape, BF16)
    return pl.pallas_call(
        backward_kernel,
        out_shape=(jax.ShapeDtypeStruct(queries.shape, BF16), out, out),
        in_specs=[smem, hbm, hbm, hbm, hbm, vmem, hbm, hbm],
        out_specs=(vmem, vmem, vmem),
        scratch_shapes=[
            pltpu.VMEM(docs.shape, jnp.int32),
            pltpu.VMEM(queries.shape, BF16),
            pltpu.VMEM(queries.shape, BF16),
            pltpu.VMEM(queries.shape, BF16),
            pltpu.VMEM(key_matrix.shape, BF16),
            pltpu.VMEM(key_matrix.shape, BF16),
            pltpu.VMEM((32, 2) + chunk, BF16),
            pltpu.VMEM((2, BLOCK, WIDTH), BF16),
            pltpu.VMEM((2, rows, 2 * WIDTH), BF16),
            pltpu.VMEM((2, rows, 2 * WIDTH), BF16),
            pltpu.VMEM((2, 2 * WIDTH, rows), BF16),
            pltpu.VMEM((2, 2 * WIDTH, rows), BF16),
            pltpu.VMEM((2, WIDTH, rows), F32),
            pltpu.VMEM((2, 2) + chunk, F32),
            pltpu.VMEM((16, 2) + chunk, F32),
            pltpu.VMEM((16, 2) + chunk, BF16),
            pltpu.VMEM((16, 2) + chunk, BF16),
            pltpu.VMEM((4, 4, 2) + chunk, BF16),
            pltpu.VMEM((2, 4, 2, BLOCK, WIDTH), BF16),
            pltpu.VMEM((4, 4, 2) + chunk, BF16),
            pltpu.VMEM((4, 2) + chunk, BF16),
            pltpu.VMEM((2, 2, BLOCK, WIDTH), BF16),
            pltpu.VMEM((2,) + chunk, F32),
            pltpu.VMEM((2, BLOCK, WIDTH), F32),
            dma((6,)),
            dma((2, 2, 4)), dma((2, 2, 4)), dma((2, 4)), dma((2, 4)), dma((4, 5)), dma((4, 5)),
            dma((5, 4)), dma((5, 4)), dma((16,)), dma((16,)), dma((4, 4)), dma((4, 4)),
            dma((2, 4)), dma((2, 4)), dma((2, 2, 4)), dma((2, 2, 4)),
        ],
        compiler_params=pltpu.CompilerParams(
            collective_id=0, has_side_effects=True, vmem_limit_bytes=56 * 2**20
        ),
        name="backward",
    )(order, docs, queries, output, grad_out, norm_turn, key_matrix, value_matrix)


def hand_out_kernel(dq_ref, dk_ref, dv_ref, dq_out, dk_out, dv_out, sem):
    pairs = ((dq_ref, dq_out), (dk_ref, dk_out), (dv_ref, dv_out))
    copies = [pltpu.make_async_copy(src, dst, sem.at[i]) for i, (src, dst) in enumerate(pairs)]
    for copy in copies:
        copy.start()
    for copy in copies:
        copy.wait()


def hand_out(*grads):
    hbm = pl.BlockSpec(memory_space=pl.ANY)
    return pl.pallas_call(
        hand_out_kernel,
        out_shape=tuple(jax.ShapeDtypeStruct(grad.shape, grad.dtype) for grad in grads),
        in_specs=[pl.BlockSpec(memory_space=pltpu.VMEM)] * 3,
        out_specs=(hbm,) * 3,
        scratch_shapes=[pltpu.SemaphoreType.DMA((3,))],
        name="hand_out",
    )(*grads)


def body(queries, key_matrix, value_matrix, output, grad_out, log_norm, doc_ids, block_order):
    grads = backward(
        block_order, doc_ids.reshape(-1, WIDTH), queries, output, grad_out, log_norm.T,
        key_matrix, value_matrix,
    )
    return hand_out(*grads)


def solution(mesh):
    placed = (
        P("blk", "head"),
        P(("blk", "head"), None),
        P(("blk", "head"), None),
        P("blk", "head"),
        P("blk", "head"),
        P("blk", "head"),
        P(),
        P(),
    )
    return jax.shard_map(
        body,
        mesh=mesh,
        in_specs=placed,
        out_specs=(P("blk", "head"), P(("blk", "head"), None), P(("blk", "head"), None)),
        check_vma=False,
    )
```

```python
import functools
import math

import jax
import jax.numpy as jnp
from jax import lax
from jax.experimental import pallas as pl
from jax.experimental.pallas import tpu as pltpu
from jax.sharding import PartitionSpec as P

WIDTH = 128
BLOCK = 64
DOCS = 6
TILE = 256
MASKED = -(2.0**17)
ROOT = math.sqrt(WIDTH)
SCALE = 1.0 / ROOT
EXP2_SCALE = SCALE * math.log2(math.e)
BF16 = jnp.bfloat16
F32 = jnp.float32


def root_parts():
    parts, rest = [], ROOT
    for _ in range(3):
        term = _to_bf16(rest)
        parts.append(term)
        rest -= term
    return parts


def _to_bf16(value):
    mantissa, exponent = math.frexp(value)
    return math.ldexp(round(mantissa * 256), exponent - 8)


ROOT_PARTS = root_parts()


class Place:
    def __init__(self):
        self.span = lax.axis_index("blk")
        self.head = lax.axis_index("head")
        self.core = self.span % 2
        self.x = (self.span // 2) % 4
        self.z = self.span // 8
        self.high, self.y = self.head // 4, self.head % 4
        self.partner = (1 - self.high) * 4 + self.y
        self.near_z = (1 + self.z % 2, (2 + 3 * self.z) % 5, 3 * (1 - self.z // 2))

    def at(self, z, dx=0, other=False):
        core = 1 - self.core if other else self.core
        return (z * 4 + (self.x + dx) % 4) * 2 + core

    def beside_y(self, d):
        return self.high * 4 + (self.y + d) % 4

    @property
    def sibling(self):
        return self.at(self.z, 0, True)


def meet(place):
    barrier = pltpu.get_barrier_semaphore()
    peers = [(place.span, place.beside_y(d)) for d in range(1, 4)]
    peers += [(place.at(z), place.head) for z in place.near_z]
    peers += [(place.at(z), place.partner) for z in (place.z,) + place.near_z]
    peers += [(place.at(place.z, dx), place.head) for dx in (1, 2, 3)]
    peers += [(place.sibling, place.head)]
    for peer in peers:
        pl.semaphore_signal(
            barrier, inc=1, device_id=peer, device_id_type=pl.DeviceIdType.MESH
        )
    pl.semaphore_wait(barrier, len(peers))


class Sent:
    def __init__(self, ref):
        self.ref = ref

    @property
    def at(self):
        return self

    def __getitem__(self, index):
        return (self.ref, index)


def copy_to(src, dst, send, recv, span, head):
    ref, index = send
    send = ref.at[index]
    return pltpu.make_async_remote_copy(
        src_ref=src, dst_ref=dst, send_sem=send, recv_sem=recv,
        device_id=(span, head), device_id_type=pl.DeviceIdType.MESH,
    )


def head_rows(head):
    return pl.ds(pl.multiple_of(head * 16, 16), 16)


def half_rows(high):
    return pl.ds(pl.multiple_of(high * BLOCK, BLOCK), BLOCK)


def head_columns(head):
    return pl.ds(pl.multiple_of(head * WIDTH, WIDTH), WIDTH)


OWN, LEFT, RIGHT, FAR = 0, 3, 1, 2
UNITS = [
    (0, OWN), (1, OWN), (2, OWN), (0, LEFT), (0, RIGHT), (0, FAR), (1, LEFT), (1, RIGHT),
    (1, FAR), (2, LEFT), (2, RIGHT), (2, FAR), (3, LEFT), (3, RIGHT), (3, FAR), (3, OWN),
]
ALL, MINE, OTHER = 0, 1, 2
ITEMS = [(0, MINE), (1, ALL), (0, OTHER), (2, ALL), (3, ALL)]
STEP_OF = {unit: step for step, unit in enumerate(UNITS)}


def backward_kernel(
    order_ref, docs_hbm, q_hbm, o_hbm, g_hbm, norm_ref, k_hbm, v_hbm,
    dq_ref, dk_ref, dv_ref,
    docs_ref, q_ref, o_ref, g_ref, k_ref, v_ref,
    kv_ref, other_ref, q_all, g_all, q_turn, g_turn, dq_turn, work,
    part, sib_out, sib, near, deep, near_out, deep_out, total, deep_sum, mine_sum,
    load_sem,
    head_send, head_recv, z_send, z_recv, x_send, x_recv, s_send, s_recv,
    p_send, p_recv, rx_send, rx_recv, rz_send, rz_recv, rh_send, rh_recv,
):
    head_send, z_send, x_send, s_send, p_send, rx_send, rz_send, rh_send = map(
        Sent, (head_send, z_send, x_send, s_send, p_send, rx_send, rz_send, rh_send)
    )
    me = Place()
    own, head = me.span, me.head
    order = (me.z,) + me.near_z
    sibling = me.sibling

    loads = [
        pltpu.make_async_copy(src, dst, load_sem.at[i])
        for i, (src, dst) in enumerate(
            (
                (k_hbm, k_ref), (v_hbm, v_ref), (q_hbm, q_ref), (g_hbm, g_ref),
                (o_hbm, o_ref), (docs_hbm, docs_ref),
            )
        )
    ]
    for load in loads:
        load.start()
    meet(me)
    loads[0].wait()
    loads[1].wait()

    sent = []

    def send(src, dst, sent_sem, recv_sem, span, to_head):
        copy_to(src, dst, sent_sem, recv_sem, span, to_head).start()
        sent.append((src.shape, sent_sem))

    def arrived(block, recv, span):
        copy_to(block, block, s_send.at[0, 0], recv, span, head).wait_recv()

    homes = (kv_ref.at[own, :, half_rows(me.high), :], other_ref)
    groups = (me.high, 1 - me.high)
    for d in range(1, 4):
        to = me.beside_y(d)
        for i, (home, group) in enumerate(zip(homes, groups)):
            columns = head_columns(group * 4 + (me.y + d) % 4)
            for j, ref in enumerate((k_ref, v_ref)):
                send(
                    ref.at[:, columns], home.at[j, head_rows(me.y), :],
                    head_send.at[i, j, d], head_recv.at[i, j, d], own, to,
                )
    for j, ref in enumerate((k_ref, v_ref)):
        kv_ref[own, j, head_rows(head), :] = ref[:, head_columns(head)]
        other_ref[j, head_rows(me.y), :] = ref[:, head_columns(me.partner)]

    for load in loads[2:]:
        load.wait()
    docs = docs_ref[...]
    starts = [jnp.sum((docs < d).astype(jnp.int32)) for d in range(1, DOCS)]
    lane = lax.broadcasted_iota(jnp.int32, (BLOCK, WIDTH), 1)
    row = lax.broadcasted_iota(jnp.int32, (BLOCK, WIDTH), 0)
    one_hot = (lane == row).astype(F32)
    norm_lane = (lane >= BLOCK) & (lane < BLOCK + 3)
    lanes = lax.broadcasted_iota(jnp.int32, (1, WIDTH), 1)
    norms = norm_ref[...].astype(F32).T
    query_pos, query_start = [], []

    def prepare(half):
        here = slice(half * BLOCK, (half + 1) * BLOCK)
        for h in range(8):
            cols = slice(h * WIDTH, (h + 1) * WIDTH)
            there = slice(h * BLOCK, (h + 1) * BLOCK)
            g = g_ref[here, cols]
            q_all[half, there, :WIDTH] = q_ref[here, cols]
            g_all[half, there, :WIDTH] = g
            norm = norms[here, h : h + 1]
            q_all[half, there, WIDTH:] = jnp.where(norm_lane, norm, one_hot).astype(BF16)
            delta = jnp.sum(g.astype(F32) * o_ref[here, cols].astype(F32), axis=1, keepdims=True)
            high = delta.astype(BF16).astype(F32)
            mid = (delta - high).astype(BF16).astype(F32)
            low = delta - high - mid
            extra = jnp.where(
                lane == 0, high, jnp.where(lane == 1, mid, jnp.where(lane == 2, low, 0.0))
            )
            g_all[half, there, WIDTH:] = extra.astype(BF16)
        q_turn[half] = q_all[half].T
        g_turn[half] = g_all[half].T
        dq_turn[half] = jnp.zeros((WIDTH, 8 * BLOCK), F32)
        pos = lanes + order_ref[2 * own + half] * BLOCK
        start = jnp.zeros_like(pos)
        for s in starts:
            start = jnp.maximum(start, jnp.where(s <= pos, s, 0))
        query_pos.append(jnp.where(lanes < BLOCK, pos, 1 << 20))
        query_start.append(jnp.where(lanes < BLOCK, start, 0))

    prepare(0)
    tile_lane = lax.broadcasted_iota(jnp.int32, (TILE, WIDTH), 1)
    value_extra = jnp.where(tile_lane < 3, -1.0, 0.0).astype(BF16)
    norm_extra = jnp.zeros((1, WIDTH), F32)
    for i, term in enumerate(ROOT_PARTS):
        norm_extra = jnp.where(lanes == BLOCK + i, -term, norm_extra)

    for d in range(1, 4):
        source = me.beside_y(4 - d)
        for i, home in enumerate(homes):
            for j in range(2):
                here = home.at[j, head_rows((me.y + 4 - d) % 4), :]
                copy_to(
                    here, here, head_send.at[i, j, d], head_recv.at[i, j, d], own, source
                ).wait_recv()

    def give_deep(k):
        if k > 0:
            send(
                homes[0], homes[0], z_send.at[0, k], z_recv.at[me.high, me.z],
                me.at(order[k]), head,
            )
        send(
            other_ref, homes[0], z_send.at[1, k], z_recv.at[me.high, me.z],
            me.at(order[k]), me.partner,
        )

    def item(i, dx, other=False):
        k, which = ITEMS[i]
        block = kv_ref.at[me.at(order[k], dx, other)]
        if which == ALL:
            return block
        return block.at[:, half_rows(me.high if which == MINE else 1 - me.high), :]

    def over(block, i, which):
        send(block, block, s_send.at[i, which], s_recv.at[i, which], sibling, head)

    def give_column(i):
        k, which = ITEMS[i]
        span = me.at(order[k])
        for high in (me.high, 1 - me.high):
            if which == ALL or (which == OTHER and high is not me.high):
                half = kv_ref.at[span, :, half_rows(high), :]
                arrived(half, z_recv.at[high, order[k]], span)
        block = item(i, OWN)
        for dx in (FAR, RIGHT, LEFT):
            send(block, block, x_send.at[dx, i], x_recv.at[dx, i], me.at(me.z, dx), head)
        over(block, i, OWN)

    def give_on(i, *steps):
        for dx in steps:
            block = item(i, dx)
            arrived(block, x_recv.at[4 - dx, i], me.at(me.z, dx))
            over(block, i, dx)

    def ready(k, dx):
        for i, (at, _) in enumerate(ITEMS):
            if at != k:
                continue
            arrived(item(i, dx, True), s_recv.at[i, dx], sibling)

    def pair(k, dx, j):
        step = STEP_OF[k, dx]
        return part[step, j] + sib[step, j].astype(F32)

    def met(k, dx):
        step = STEP_OF[k, dx]
        arrived(sib.at[step], p_recv.at[step], sibling)

    def give_sum(step):
        k, dx = UNITS[step]
        met(k, dx)
        for j in range(2):
            near_out[dx, k, j] = pair(k, dx, j).astype(BF16)
        send(
            near_out.at[dx, k], near.at[dx, k], rx_send.at[dx, k], rx_recv.at[dx, k],
            me.at(me.z, dx), head,
        )

    def sum_column(k):
        met(k, OWN)
        sums = [pair(k, OWN, j) for j in range(2)]
        for dx in (LEFT, RIGHT, FAR):
            arrived(near.at[dx, k], rx_recv.at[dx, k], me.at(me.z, 4 - dx))
            sums = [sums[j] + near[dx, k, j].astype(F32) for j in range(2)]
        for j in range(2):
            deep_out[k, j] = sums[j].astype(BF16)
        if k == 0:
            for j in range(2):
                deep_sum[j] = sums[j]
                mine_sum[j] = deep_sum[j, half_rows(me.high), :]
        for i, to in enumerate((head, me.partner)):
            if k > 0 or i > 0:
                send(
                    deep_out.at[k, :, half_rows(me.high if i == 0 else 1 - me.high), :],
                    deep.at[me.high, me.z], rz_send.at[i, k], rz_recv.at[me.high, me.z],
                    me.at(order[k]), to,
                )

    before = {
        0: [(give_column, 1), (give_column, 2)],
        1: [(give_on, 0, LEFT, RIGHT), (give_column, 3)],
        2: [(give_on, 0, FAR), (give_column, 4)],
        3: [(give_on, 2, LEFT, RIGHT), (give_on, 1, LEFT, RIGHT)],
        4: [(give_on, 2, FAR), (give_on, 1, FAR)],
        5: [(give_sum, 3)],
        6: [(give_sum, 4)],
        7: [(give_sum, 5), (give_on, 3, LEFT, RIGHT)],
        8: [(give_sum, 6), (give_on, 3, FAR)],
        9: [(give_sum, 7)],
        10: [(give_sum, 8), (give_on, 4, LEFT, RIGHT)],
        11: [(give_sum, 9), (give_on, 4, FAR)],
        12: [(give_sum, 10)],
        13: [(give_sum, 11), (sum_column, 0)],
        14: [(give_sum, 12)],
        15: [(give_sum, 13), (sum_column, 1)],
    }
    chips = [order[k] * 4 + (me.x + dx) % 4 for k, dx in UNITS]
    give_deep(1)
    give_deep(0)
    give_column(0)
    prepare(1)
    give_deep(2)
    give_deep(3)
    block_row = lax.broadcasted_iota(jnp.int32, (BLOCK, WIDTH), 0)

    def unit(step, carry):
        for at, (k, dx) in enumerate(UNITS):

            @pl.when(step == at)
            def _():
                for action, *which in before.get(at, []):
                    action(*which)
                ready(k, dx)

        chip = chips[0]
        for at in range(1, len(UNITS)):
            chip = jnp.where(step == at, chips[at], chip)
        keys = kv_ref[pl.ds(2 * chip, 2), 0].reshape(TILE, WIDTH)
        values = kv_ref[pl.ds(2 * chip, 2), 1].reshape(TILE, WIDTH)
        key_pos = jnp.concatenate(
            [block_row + order_ref[4 * chip + i] * BLOCK for i in range(4)], axis=0
        )
        value_side = jnp.concatenate([values, value_extra], axis=1)
        keys_turn = keys.T
        scores, grad_weights = [], []
        for half in range(2):
            hidden = (key_pos > query_pos[half]) | (key_pos < query_start[half])
            extra = jnp.where(hidden, MASKED, norm_extra).astype(BF16)
            scores.append(
                jnp.dot(
                    jnp.concatenate([keys, extra], axis=1), q_turn[half],
                    preferred_element_type=F32,
                )
            )
            grad_weights.append(jnp.dot(value_side, g_turn[half], preferred_element_type=F32))
        weights = [jnp.exp2(score * EXP2_SCALE) for score in scores]
        grad_scores = [(weights[half] * grad_weights[half]).astype(BF16) for half in range(2)]
        grad_values = sum(
            jnp.dot(weights[half].astype(BF16), g_all[half, :, :WIDTH], preferred_element_type=F32)
            for half in range(2)
        )
        grad_keys = sum(
            jnp.dot(grad_scores[half], q_all[half, :, :WIDTH], preferred_element_type=F32)
            for half in range(2)
        )
        for half in range(2):
            dq_turn[half] += jnp.dot(keys_turn, grad_scores[half], preferred_element_type=F32)
        for i in range(2):
            rows = slice(2 * i * BLOCK, 2 * (i + 1) * BLOCK)
            work[i, 0] = grad_keys[rows] * SCALE
            work[i, 1] = grad_values[rows]
        part[step] = work[me.core]
        sib_out[step] = work[1 - me.core].astype(BF16)
        copy_to(
            sib_out.at[step], sib.at[step], p_send.at[step], p_recv.at[step], sibling, head
        ).start()
        return carry

    lax.fori_loop(0, len(UNITS), unit, 0)
    give_sum(14)
    sum_column(2)
    for half in range(2):
        dq = (dq_turn[half] * SCALE).T
        for h in range(8):
            dq_ref[half * BLOCK : (half + 1) * BLOCK, h * WIDTH : (h + 1) * WIDTH] = dq[
                h * BLOCK : (h + 1) * BLOCK
            ].astype(BF16)
    sum_column(3)
    for i, group in enumerate(groups):
        sums = None if i else [mine_sum[j] for j in range(2)]
        for z in order[1 - i :]:
            arrived(deep.at[group, z], rz_recv.at[group, z], me.at(z))
            got = [deep[group, z, j].astype(F32) for j in range(2)]
            sums = got if sums is None else [sums[j] + got[j] for j in range(2)]
        for j in range(2):
            total[i, j] = sums[j].astype(BF16)
    outs = (dk_ref, dv_ref)
    for d in range(1, 4):
        for i, group in enumerate(groups):
            columns = head_columns(group * 4 + me.y)
            for j in range(2):
                send(
                    total.at[i, j, head_rows((me.y + d) % 4), :], outs[j].at[:, columns],
                    rh_send.at[i, j, d], rh_recv.at[i, j, d], own, me.beside_y(d),
                )
    for i, group in enumerate(groups):
        for j in range(2):
            outs[j][:, head_columns(group * 4 + me.y)] = total[i, j, head_rows(me.y), :]
    for d in range(1, 4):
        for i, group in enumerate(groups):
            for j in range(2):
                here = outs[j].at[:, head_columns(group * 4 + (me.y + 4 - d) % 4)]
                copy_to(
                    here, here, rh_send.at[i, j, d], rh_recv.at[i, j, d], own, me.beside_y(4 - d)
                ).wait_recv()
    sent += [(sib_out.shape[1:], p_send.at[step]) for step in range(len(UNITS))]
    shapes = {
        (2, 2 * BLOCK, WIDTH): kv_ref.at[0],
        (2 * BLOCK, WIDTH): kv_ref.at[0, 0],
        (2, BLOCK, WIDTH): other_ref,
        (BLOCK, WIDTH): other_ref.at[0],
        (16, WIDTH): kv_ref.at[0, 0, pl.ds(0, 16), :],
    }
    for shape, sent_sem in sent:
        block = shapes[tuple(shape)]
        copy_to(block, block, sent_sem, s_recv.at[0, 0], sibling, head).wait_send()


def backward(order, docs, queries, output, grad_out, norm_turn, key_matrix, value_matrix):
    smem = pl.BlockSpec(memory_space=pltpu.SMEM)
    vmem = pl.BlockSpec(memory_space=pltpu.VMEM)
    hbm = pl.BlockSpec(memory_space=pl.ANY)
    dma = pltpu.SemaphoreType.DMA
    chunk = (2 * BLOCK, WIDTH)
    rows = 8 * BLOCK
    out = jax.ShapeDtypeStruct(key_matrix.shape, BF16)
    return pl.pallas_call(
        backward_kernel,
        out_shape=(jax.ShapeDtypeStruct(queries.shape, BF16), out, out),
        in_specs=[smem, hbm, hbm, hbm, hbm, vmem, hbm, hbm],
        out_specs=(vmem, vmem, vmem),
        scratch_shapes=[
            pltpu.VMEM(docs.shape, jnp.int32),
            pltpu.VMEM(queries.shape, BF16),
            pltpu.VMEM(queries.shape, BF16),
            pltpu.VMEM(queries.shape, BF16),
            pltpu.VMEM(key_matrix.shape, BF16),
            pltpu.VMEM(key_matrix.shape, BF16),
            pltpu.VMEM((32, 2) + chunk, BF16),
            pltpu.VMEM((2, BLOCK, WIDTH), BF16),
            pltpu.VMEM((2, rows, 2 * WIDTH), BF16),
            pltpu.VMEM((2, rows, 2 * WIDTH), BF16),
            pltpu.VMEM((2, 2 * WIDTH, rows), BF16),
            pltpu.VMEM((2, 2 * WIDTH, rows), BF16),
            pltpu.VMEM((2, WIDTH, rows), F32),
            pltpu.VMEM((2, 2) + chunk, F32),
            pltpu.VMEM((16, 2) + chunk, F32),
            pltpu.VMEM((16, 2) + chunk, BF16),
            pltpu.VMEM((16, 2) + chunk, BF16),
            pltpu.VMEM((4, 4, 2) + chunk, BF16),
            pltpu.VMEM((2, 4, 2, BLOCK, WIDTH), BF16),
            pltpu.VMEM((4, 4, 2) + chunk, BF16),
            pltpu.VMEM((4, 2) + chunk, BF16),
            pltpu.VMEM((2, 2, BLOCK, WIDTH), BF16),
            pltpu.VMEM((2,) + chunk, F32),
            pltpu.VMEM((2, BLOCK, WIDTH), F32),
            dma((6,)),
            dma((2, 2, 4)), dma((2, 2, 4)), dma((2, 4)), dma((2, 4)), dma((4, 5)), dma((4, 5)),
            dma((5, 4)), dma((5, 4)), dma((16,)), dma((16,)), dma((4, 4)), dma((4, 4)),
            dma((2, 4)), dma((2, 4)), dma((2, 2, 4)), dma((2, 2, 4)),
        ],
        compiler_params=pltpu.CompilerParams(
            collective_id=0, has_side_effects=True, vmem_limit_bytes=56 * 2**20
        ),
        name="backward",
    )(order, docs, queries, output, grad_out, norm_turn, key_matrix, value_matrix)


def hand_out_kernel(dq_ref, dk_ref, dv_ref, dq_out, dk_out, dv_out, sem):
    pairs = ((dq_ref, dq_out), (dk_ref, dk_out), (dv_ref, dv_out))
    copies = [pltpu.make_async_copy(src, dst, sem.at[i]) for i, (src, dst) in enumerate(pairs)]
    for copy in copies:
        copy.start()
    for copy in copies:
        copy.wait()


def hand_out(*grads):
    hbm = pl.BlockSpec(memory_space=pl.ANY)
    return pl.pallas_call(
        hand_out_kernel,
        out_shape=tuple(jax.ShapeDtypeStruct(grad.shape, grad.dtype) for grad in grads),
        in_specs=[pl.BlockSpec(memory_space=pltpu.VMEM)] * 3,
        out_specs=(hbm,) * 3,
        scratch_shapes=[pltpu.SemaphoreType.DMA((3,))],
        name="hand_out",
    )(*grads)


def body(queries, key_matrix, value_matrix, output, grad_out, log_norm, doc_ids, block_order):
    grads = backward(
        block_order, doc_ids.reshape(-1, WIDTH), queries, output, grad_out, log_norm.T,
        key_matrix, value_matrix,
    )
    return hand_out(*grads)


def solution(mesh):
    placed = (
        P("blk", "head"),
        P(("blk", "head"), None),
        P(("blk", "head"), None),
        P("blk", "head"),
        P("blk", "head"),
        P("blk", "head"),
        P(),
        P(),
    )
    return jax.shard_map(
        body,
        mesh=mesh,
        in_specs=placed,
        out_specs=(P("blk", "head"), P(("blk", "head"), None), P(("blk", "head"), None)),
        check_vma=False,
    )
```

```python
import functools
import math

import jax
import jax.numpy as jnp
from jax import lax
from jax.experimental import pallas as pl
from jax.experimental.pallas import tpu as pltpu
from jax.sharding import PartitionSpec as P

WIDTH = 128
BLOCK = 64
DOCS = 6
TILE = 256
MASKED = -(2.0**17)
ROOT = math.sqrt(WIDTH)
SCALE = 1.0 / ROOT
EXP2_SCALE = SCALE * math.log2(math.e)
BF16 = jnp.bfloat16
F32 = jnp.float32


def root_parts():
    parts, rest = [], ROOT
    for _ in range(3):
        term = _to_bf16(rest)
        parts.append(term)
        rest -= term
    return parts


def _to_bf16(value):
    mantissa, exponent = math.frexp(value)
    return math.ldexp(round(mantissa * 256), exponent - 8)


ROOT_PARTS = root_parts()


class Place:
    def __init__(self):
        self.span = lax.axis_index("blk")
        self.head = lax.axis_index("head")
        self.core = self.span % 2
        self.x = (self.span // 2) % 4
        self.z = self.span // 8
        self.high, self.y = self.head // 4, self.head % 4
        self.partner = (1 - self.high) * 4 + self.y
        self.near_z = (1 + self.z % 2, (2 + 3 * self.z) % 5, 3 * (1 - self.z // 2))

    def at(self, z, dx=0, other=False):
        core = 1 - self.core if other else self.core
        return (z * 4 + (self.x + dx) % 4) * 2 + core

    def beside_y(self, d):
        return self.high * 4 + (self.y + d) % 4

    @property
    def sibling(self):
        return self.at(self.z, 0, True)


def meet(place):
    barrier = pltpu.get_barrier_semaphore()
    peers = [(place.span, place.beside_y(d)) for d in range(1, 4)]
    peers += [(place.at(z), place.head) for z in place.near_z]
    peers += [(place.at(z), place.partner) for z in (place.z,) + place.near_z]
    peers += [(place.at(place.z, dx), place.head) for dx in (1, 2, 3)]
    peers += [(place.sibling, place.head)]
    for peer in peers:
        pl.semaphore_signal(
            barrier, inc=1, device_id=peer, device_id_type=pl.DeviceIdType.MESH
        )
    return lambda: pl.semaphore_wait(barrier, len(peers))


class Sent:
    def __init__(self, ref):
        self.ref = ref

    @property
    def at(self):
        return self

    def __getitem__(self, index):
        return (self.ref, index)


def copy_to(src, dst, send, recv, span, head):
    ref, index = send
    send = ref.at[index]
    return pltpu.make_async_remote_copy(
        src_ref=src, dst_ref=dst, send_sem=send, recv_sem=recv,
        device_id=(span, head), device_id_type=pl.DeviceIdType.MESH,
    )


def head_rows(head):
    return pl.ds(pl.multiple_of(head * 16, 16), 16)


def half_rows(high):
    return pl.ds(pl.multiple_of(high * BLOCK, BLOCK), BLOCK)


def head_columns(head):
    return pl.ds(pl.multiple_of(head * WIDTH, WIDTH), WIDTH)


OWN, LEFT, RIGHT, FAR = 0, 3, 1, 2
UNITS = [
    (0, OWN), (1, OWN), (2, OWN), (0, LEFT), (0, RIGHT), (0, FAR), (1, LEFT), (1, RIGHT),
    (1, FAR), (2, LEFT), (2, RIGHT), (2, FAR), (3, LEFT), (3, RIGHT), (3, FAR), (3, OWN),
]
ALL, MINE, OTHER = 0, 1, 2
ITEMS = [(0, MINE), (1, ALL), (0, OTHER), (2, ALL), (3, ALL)]
STEP_OF = {unit: step for step, unit in enumerate(UNITS)}


def backward_kernel(
    order_ref, docs_hbm, q_hbm, o_hbm, g_hbm, norm_ref, k_hbm, v_hbm,
    dq_ref, dk_ref, dv_ref,
    docs_ref, q_ref, o_ref, g_ref, k_ref, v_ref,
    kv_ref, other_ref, q_all, g_all, q_turn, g_turn, dq_turn, work,
    part, sib_out, sib, near, deep, near_out, deep_out, total, deep_sum, mine_sum,
    load_sem,
    head_send, head_recv, z_send, z_recv, x_send, x_recv, s_send, s_recv,
    p_send, p_recv, rx_send, rx_recv, rz_send, rz_recv, rh_send, rh_recv,
):
    head_send, z_send, x_send, s_send, p_send, rx_send, rz_send, rh_send = map(
        Sent, (head_send, z_send, x_send, s_send, p_send, rx_send, rz_send, rh_send)
    )
    me = Place()
    own, head = me.span, me.head
    order = (me.z,) + me.near_z
    sibling = me.sibling

    all_here = meet(me)
    loads = [
        pltpu.make_async_copy(src, dst, load_sem.at[i])
        for i, (src, dst) in enumerate(
            (
                (k_hbm, k_ref), (v_hbm, v_ref), (q_hbm, q_ref), (g_hbm, g_ref),
                (o_hbm, o_ref), (docs_hbm, docs_ref),
            )
        )
    ]
    for load in loads:
        load.start()
    all_here()
    loads[0].wait()
    loads[1].wait()

    sent = []

    def send(src, dst, sent_sem, recv_sem, span, to_head):
        copy_to(src, dst, sent_sem, recv_sem, span, to_head).start()
        sent.append((src.shape, sent_sem))

    def arrived(block, recv, span):
        copy_to(block, block, s_send.at[0, 0], recv, span, head).wait_recv()

    homes = (kv_ref.at[own, :, half_rows(me.high), :], other_ref)
    groups = (me.high, 1 - me.high)
    for d in range(1, 4):
        to = me.beside_y(d)
        for i, (home, group) in enumerate(zip(homes, groups)):
            columns = head_columns(group * 4 + (me.y + d) % 4)
            for j, ref in enumerate((k_ref, v_ref)):
                send(
                    ref.at[:, columns], home.at[j, head_rows(me.y), :],
                    head_send.at[i, j, d], head_recv.at[i, j, d], own, to,
                )
    for j, ref in enumerate((k_ref, v_ref)):
        kv_ref[own, j, head_rows(head), :] = ref[:, head_columns(head)]
        other_ref[j, head_rows(me.y), :] = ref[:, head_columns(me.partner)]

    for d in range(1, 4):
        source = me.beside_y(4 - d)
        for i, home in enumerate(homes):
            for j in range(2):
                here = home.at[j, head_rows((me.y + 4 - d) % 4), :]
                copy_to(
                    here, here, head_send.at[i, j, d], head_recv.at[i, j, d], own, source
                ).wait_recv()

    def give_deep(k):
        if k > 0:
            send(
                homes[0], homes[0], z_send.at[0, k], z_recv.at[me.high, me.z],
                me.at(order[k]), head,
            )
        send(
            other_ref, homes[0], z_send.at[1, k], z_recv.at[me.high, me.z],
            me.at(order[k]), me.partner,
        )

    def item(i, dx, other=False):
        k, which = ITEMS[i]
        block = kv_ref.at[me.at(order[k], dx, other)]
        if which == ALL:
            return block
        return block.at[:, half_rows(me.high if which == MINE else 1 - me.high), :]

    def over(block, i, which):
        send(block, block, s_send.at[i, which], s_recv.at[i, which], sibling, head)

    def give_column(i):
        k, which = ITEMS[i]
        span = me.at(order[k])
        for high in (me.high, 1 - me.high):
            if which == ALL or (which == OTHER and high is not me.high):
                half = kv_ref.at[span, :, half_rows(high), :]
                arrived(half, z_recv.at[high, order[k]], span)
        block = item(i, OWN)
        for dx in (FAR, RIGHT, LEFT):
            send(block, block, x_send.at[dx, i], x_recv.at[dx, i], me.at(me.z, dx), head)
        over(block, i, OWN)

    def give_on(i, *steps):
        for dx in steps:
            block = item(i, dx)
            arrived(block, x_recv.at[4 - dx, i], me.at(me.z, dx))
            over(block, i, dx)

    def ready(k, dx):
        for i, (at, _) in enumerate(ITEMS):
            if at != k:
                continue
            arrived(item(i, dx, True), s_recv.at[i, dx], sibling)

    def pair(k, dx, j):
        step = STEP_OF[k, dx]
        return part[step, j] + sib[step, j].astype(F32)

    def met(k, dx):
        step = STEP_OF[k, dx]
        arrived(sib.at[step], p_recv.at[step], sibling)

    def give_sum(step):
        k, dx = UNITS[step]
        met(k, dx)
        for j in range(2):
            near_out[dx, k, j] = pair(k, dx, j).astype(BF16)
        send(
            near_out.at[dx, k], near.at[dx, k], rx_send.at[dx, k], rx_recv.at[dx, k],
            me.at(me.z, dx), head,
        )

    def sum_column(k):
        met(k, OWN)
        sums = [pair(k, OWN, j) for j in range(2)]
        for dx in (LEFT, RIGHT, FAR):
            arrived(near.at[dx, k], rx_recv.at[dx, k], me.at(me.z, 4 - dx))
            sums = [sums[j] + near[dx, k, j].astype(F32) for j in range(2)]
        for j in range(2):
            deep_out[k, j] = sums[j].astype(BF16)
        if k == 0:
            for j in range(2):
                deep_sum[j] = sums[j]
                mine_sum[j] = deep_sum[j, half_rows(me.high), :]
        for i, to in enumerate((head, me.partner)):
            if k > 0 or i > 0:
                send(
                    deep_out.at[k, :, half_rows(me.high if i == 0 else 1 - me.high), :],
                    deep.at[me.high, me.z], rz_send.at[i, k], rz_recv.at[me.high, me.z],
                    me.at(order[k]), to,
                )

    before = {
        0: [(give_column, 1), (give_column, 2)],
        1: [(give_on, 0, LEFT, RIGHT), (give_column, 3)],
        2: [(give_on, 0, FAR), (give_column, 4)],
        3: [(give_on, 2, LEFT, RIGHT), (give_on, 1, LEFT, RIGHT)],
        4: [(give_on, 2, FAR), (give_on, 1, FAR)],
        5: [(give_sum, 3)],
        6: [(give_sum, 4)],
        7: [(give_sum, 5), (give_on, 3, LEFT, RIGHT)],
        8: [(give_sum, 6), (give_on, 3, FAR)],
        9: [(give_sum, 7)],
        10: [(give_sum, 8), (give_on, 4, LEFT, RIGHT)],
        11: [(give_sum, 9), (give_on, 4, FAR)],
        12: [(give_sum, 10)],
        13: [(give_sum, 11), (sum_column, 0)],
        14: [(give_sum, 12)],
        15: [(give_sum, 13), (sum_column, 1)],
    }
    chips = [order[k] * 4 + (me.x + dx) % 4 for k, dx in UNITS]
    give_deep(1)
    give_deep(0)
    give_column(0)
    for load in loads[2:]:
        load.wait()
    docs = docs_ref[...]
    starts = [jnp.sum((docs < d).astype(jnp.int32)) for d in range(1, DOCS)]
    lane = lax.broadcasted_iota(jnp.int32, (BLOCK, WIDTH), 1)
    row = lax.broadcasted_iota(jnp.int32, (BLOCK, WIDTH), 0)
    one_hot = (lane == row).astype(F32)
    norm_lane = (lane >= BLOCK) & (lane < BLOCK + 3)
    lanes = lax.broadcasted_iota(jnp.int32, (1, WIDTH), 1)
    norms = norm_ref[...].astype(F32).T
    query_pos, query_start = [], []

    def prepare(half):
        here = slice(half * BLOCK, (half + 1) * BLOCK)
        for h in range(8):
            cols = slice(h * WIDTH, (h + 1) * WIDTH)
            there = slice(h * BLOCK, (h + 1) * BLOCK)
            g = g_ref[here, cols]
            q_all[half, there, :WIDTH] = q_ref[here, cols]
            g_all[half, there, :WIDTH] = g
            norm = norms[here, h : h + 1]
            q_all[half, there, WIDTH:] = jnp.where(norm_lane, norm, one_hot).astype(BF16)
            delta = jnp.sum(g.astype(F32) * o_ref[here, cols].astype(F32), axis=1, keepdims=True)
            high = delta.astype(BF16).astype(F32)
            mid = (delta - high).astype(BF16).astype(F32)
            low = delta - high - mid
            extra = jnp.where(
                lane == 0, high, jnp.where(lane == 1, mid, jnp.where(lane == 2, low, 0.0))
            )
            g_all[half, there, WIDTH:] = extra.astype(BF16)
        q_turn[half] = q_all[half].T
        g_turn[half] = g_all[half].T
        dq_turn[half] = jnp.zeros((WIDTH, 8 * BLOCK), F32)
        pos = lanes + order_ref[2 * own + half] * BLOCK
        start = jnp.zeros_like(pos)
        for s in starts:
            start = jnp.maximum(start, jnp.where(s <= pos, s, 0))
        query_pos.append(jnp.where(lanes < BLOCK, pos, 1 << 20))
        query_start.append(jnp.where(lanes < BLOCK, start, 0))

    prepare(0)
    give_deep(2)
    give_deep(3)
    prepare(1)
    tile_lane = lax.broadcasted_iota(jnp.int32, (TILE, WIDTH), 1)
    value_extra = jnp.where(tile_lane < 3, -1.0, 0.0).astype(BF16)
    norm_extra = jnp.zeros((1, WIDTH), F32)
    for i, term in enumerate(ROOT_PARTS):
        norm_extra = jnp.where(lanes == BLOCK + i, -term, norm_extra)

    block_row = lax.broadcasted_iota(jnp.int32, (BLOCK, WIDTH), 0)

    def unit(step, carry):
        for at, (k, dx) in enumerate(UNITS):

            @pl.when(step == at)
            def _():
                for action, *which in before.get(at, []):
                    action(*which)
                ready(k, dx)

        chip = chips[0]
        for at in range(1, len(UNITS)):
            chip = jnp.where(step == at, chips[at], chip)
        keys = kv_ref[pl.ds(2 * chip, 2), 0].reshape(TILE, WIDTH)
        values = kv_ref[pl.ds(2 * chip, 2), 1].reshape(TILE, WIDTH)
        key_pos = jnp.concatenate(
            [block_row + order_ref[4 * chip + i] * BLOCK for i in range(4)], axis=0
        )
        value_side = jnp.concatenate([values, value_extra], axis=1)
        keys_turn = keys.T
        scores, grad_weights = [], []
        for half in range(2):
            hidden = (key_pos > query_pos[half]) | (key_pos < query_start[half])
            extra = jnp.where(hidden, MASKED, norm_extra).astype(BF16)
            scores.append(
                jnp.dot(
                    jnp.concatenate([keys, extra], axis=1), q_turn[half],
                    preferred_element_type=F32,
                )
            )
            grad_weights.append(jnp.dot(value_side, g_turn[half], preferred_element_type=F32))
        weights = [jnp.exp2(score * EXP2_SCALE) for score in scores]
        grad_scores = [(weights[half] * grad_weights[half]).astype(BF16) for half in range(2)]
        grad_values = sum(
            jnp.dot(weights[half].astype(BF16), g_all[half, :, :WIDTH], preferred_element_type=F32)
            for half in range(2)
        )
        grad_keys = sum(
            jnp.dot(grad_scores[half], q_all[half, :, :WIDTH], preferred_element_type=F32)
            for half in range(2)
        )
        for half in range(2):
            dq_turn[half] += jnp.dot(keys_turn, grad_scores[half], preferred_element_type=F32)
        for i in range(2):
            rows = slice(2 * i * BLOCK, 2 * (i + 1) * BLOCK)
            work[i, 0] = grad_keys[rows] * SCALE
            work[i, 1] = grad_values[rows]
        part[step] = work[me.core]
        sib_out[step] = work[1 - me.core].astype(BF16)
        copy_to(
            sib_out.at[step], sib.at[step], p_send.at[step], p_recv.at[step], sibling, head
        ).start()
        return carry

    lax.fori_loop(0, len(UNITS), unit, 0)
    give_sum(14)
    sum_column(2)
    for half in range(2):
        dq = (dq_turn[half] * SCALE).T
        for h in range(8):
            dq_ref[half * BLOCK : (half + 1) * BLOCK, h * WIDTH : (h + 1) * WIDTH] = dq[
                h * BLOCK : (h + 1) * BLOCK
            ].astype(BF16)
    sum_column(3)
    for i, group in enumerate(groups):
        sums = None if i else [mine_sum[j] for j in range(2)]
        for z in order[1 - i :]:
            arrived(deep.at[group, z], rz_recv.at[group, z], me.at(z))
            got = [deep[group, z, j].astype(F32) for j in range(2)]
            sums = got if sums is None else [sums[j] + got[j] for j in range(2)]
        for j in range(2):
            total[i, j] = sums[j].astype(BF16)
    outs = (dk_ref, dv_ref)
    for d in range(1, 4):
        for i, group in enumerate(groups):
            columns = head_columns(group * 4 + me.y)
            for j in range(2):
                send(
                    total.at[i, j, head_rows((me.y + d) % 4), :], outs[j].at[:, columns],
                    rh_send.at[i, j, d], rh_recv.at[i, j, d], own, me.beside_y(d),
                )
    for i, group in enumerate(groups):
        for j in range(2):
            outs[j][:, head_columns(group * 4 + me.y)] = total[i, j, head_rows(me.y), :]
    for d in range(1, 4):
        for i, group in enumerate(groups):
            for j in range(2):
                here = outs[j].at[:, head_columns(group * 4 + (me.y + 4 - d) % 4)]
                copy_to(
                    here, here, rh_send.at[i, j, d], rh_recv.at[i, j, d], own, me.beside_y(4 - d)
                ).wait_recv()
    sent += [(sib_out.shape[1:], p_send.at[step]) for step in range(len(UNITS))]
    shapes = {
        (2, 2 * BLOCK, WIDTH): kv_ref.at[0],
        (2 * BLOCK, WIDTH): kv_ref.at[0, 0],
        (2, BLOCK, WIDTH): other_ref,
        (BLOCK, WIDTH): other_ref.at[0],
        (16, WIDTH): kv_ref.at[0, 0, pl.ds(0, 16), :],
    }
    for shape, sent_sem in sent:
        block = shapes[tuple(shape)]
        copy_to(block, block, sent_sem, s_recv.at[0, 0], sibling, head).wait_send()


def backward(order, docs, queries, output, grad_out, norm_turn, key_matrix, value_matrix):
    smem = pl.BlockSpec(memory_space=pltpu.SMEM)
    vmem = pl.BlockSpec(memory_space=pltpu.VMEM)
    hbm = pl.BlockSpec(memory_space=pl.ANY)
    dma = pltpu.SemaphoreType.DMA
    chunk = (2 * BLOCK, WIDTH)
    rows = 8 * BLOCK
    out = jax.ShapeDtypeStruct(key_matrix.shape, BF16)
    return pl.pallas_call(
        backward_kernel,
        out_shape=(jax.ShapeDtypeStruct(queries.shape, BF16), out, out),
        in_specs=[smem, hbm, hbm, hbm, hbm, vmem, hbm, hbm],
        out_specs=(vmem, vmem, vmem),
        scratch_shapes=[
            pltpu.VMEM(docs.shape, jnp.int32),
            pltpu.VMEM(queries.shape, BF16),
            pltpu.VMEM(queries.shape, BF16),
            pltpu.VMEM(queries.shape, BF16),
            pltpu.VMEM(key_matrix.shape, BF16),
            pltpu.VMEM(key_matrix.shape, BF16),
            pltpu.VMEM((32, 2) + chunk, BF16),
            pltpu.VMEM((2, BLOCK, WIDTH), BF16),
            pltpu.VMEM((2, rows, 2 * WIDTH), BF16),
            pltpu.VMEM((2, rows, 2 * WIDTH), BF16),
            pltpu.VMEM((2, 2 * WIDTH, rows), BF16),
            pltpu.VMEM((2, 2 * WIDTH, rows), BF16),
            pltpu.VMEM((2, WIDTH, rows), F32),
            pltpu.VMEM((2, 2) + chunk, F32),
            pltpu.VMEM((16, 2) + chunk, F32),
            pltpu.VMEM((16, 2) + chunk, BF16),
            pltpu.VMEM((16, 2) + chunk, BF16),
            pltpu.VMEM((4, 4, 2) + chunk, BF16),
            pltpu.VMEM((2, 4, 2, BLOCK, WIDTH), BF16),
            pltpu.VMEM((4, 4, 2) + chunk, BF16),
            pltpu.VMEM((4, 2) + chunk, BF16),
            pltpu.VMEM((2, 2, BLOCK, WIDTH), BF16),
            pltpu.VMEM((2,) + chunk, F32),
            pltpu.VMEM((2, BLOCK, WIDTH), F32),
            dma((6,)),
            dma((2, 2, 4)), dma((2, 2, 4)), dma((2, 4)), dma((2, 4)), dma((4, 5)), dma((4, 5)),
            dma((5, 4)), dma((5, 4)), dma((16,)), dma((16,)), dma((4, 4)), dma((4, 4)),
            dma((2, 4)), dma((2, 4)), dma((2, 2, 4)), dma((2, 2, 4)),
        ],
        compiler_params=pltpu.CompilerParams(
            collective_id=0, has_side_effects=True, vmem_limit_bytes=56 * 2**20
        ),
        name="backward",
    )(order, docs, queries, output, grad_out, norm_turn, key_matrix, value_matrix)


def hand_out_kernel(dq_ref, dk_ref, dv_ref, dq_out, dk_out, dv_out, sem):
    pairs = ((dq_ref, dq_out), (dk_ref, dk_out), (dv_ref, dv_out))
    copies = [pltpu.make_async_copy(src, dst, sem.at[i]) for i, (src, dst) in enumerate(pairs)]
    for copy in copies:
        copy.start()
    for copy in copies:
        copy.wait()


def hand_out(*grads):
    hbm = pl.BlockSpec(memory_space=pl.ANY)
    return pl.pallas_call(
        hand_out_kernel,
        out_shape=tuple(jax.ShapeDtypeStruct(grad.shape, grad.dtype) for grad in grads),
        in_specs=[pl.BlockSpec(memory_space=pltpu.VMEM)] * 3,
        out_specs=(hbm,) * 3,
        scratch_shapes=[pltpu.SemaphoreType.DMA((3,))],
        name="hand_out",
    )(*grads)


def body(queries, key_matrix, value_matrix, output, grad_out, log_norm, doc_ids, block_order):
    grads = backward(
        block_order, doc_ids.reshape(-1, WIDTH), queries, output, grad_out, log_norm.T,
        key_matrix, value_matrix,
    )
    return hand_out(*grads)


def solution(mesh):
    placed = (
        P("blk", "head"),
        P(("blk", "head"), None),
        P(("blk", "head"), None),
        P("blk", "head"),
        P("blk", "head"),
        P("blk", "head"),
        P(),
        P(),
    )
    return jax.shard_map(
        body,
        mesh=mesh,
        in_specs=placed,
        out_specs=(P("blk", "head"), P(("blk", "head"), None), P(("blk", "head"), None)),
        check_vma=False,
    )
```
